128 devices in a mesh: shot: 8 (over z_lo, y), rcv: 16 (over x, z_hi, core).
Axes of the slice: x: 4, y: 4, z: 4 (z_hi: 2, z_lo: 2; z = z_hi * 2 + z_lo), core: 2. Of those that a mesh axis runs over, the one named last changes fastest.
Arguments:
- traces: bfloat16 [512, 1024, 2048], P('shot', 'rcv'), may hold values from -6 to 6
- phases: int32 [512, 64], P('shot'), may hold values from 0 to 63
- bins: int32 [256], replicated, may hold values from 1 to 1023
- observed: float32 [64, 2, 1024, 256], P('shot', None, 'rcv'), may hold values from -6 to 6
Outputs:
- residual_traces: float32 [64, 1024, 2048], P('shot', None, 'rcv')
The draws below stay inside these ranges and needn't reach their ends.
All inputs are finite; a program needn't handle non-finite values.
Results may differ from the reference program's by a relative error of at most 0.0015.
Values sent between devices are 32-bit elements; how exact they have to be, the bound alone decides.
A program may use at most 128 MiB of HBM per device.

```python
import math
import jax
import jax.numpy as jnp
from jax import lax

NT = 2048
F = 256
E = 64
SHOTS = 512
NR = 1024


def set_ends(drawn, rng, least, top_value):
    index_at = [jax.random.randint(jax.random.fold_in(rng, axis), (), 0, length) for axis, length in enumerate(drawn.shape)]
    longest = drawn.shape.index(max(drawn.shape))
    next_to = index_at[:longest] + [(index_at[longest] + 1) % drawn.shape[longest]] + index_at[longest + 1:]
    return drawn.at[tuple(index_at)].set(least).at[tuple(next_to)].set(top_value)


def block_scale(stream_key, extent, shards, least, largest):
    level, own = 1.0, jax.random.fold_in(stream_key, 6)
    for axis_at, parts in shards:
        draws = jnp.exp(jax.random.uniform(jax.random.fold_in(own, axis_at), (parts,), jnp.float32, least / len(shards), largest / len(shards)))
        level = level * jnp.repeat(draws, extent[axis_at] // parts).reshape([-1 if axis == axis_at else 1 for axis in range(len(extent))])
    return level


def gaussian(stream_key, dims, spread, reach, pieces=(), kind=jnp.bfloat16):
    entries = spread * jax.random.normal(stream_key, dims, jnp.float32)
    if pieces:
        entries = entries * block_scale(stream_key, dims, pieces, -0.22, 0.18)
    return jnp.clip(entries, -reach, reach).astype(kind)


def setup_inputs(seed: int = 0) -> dict:
    arg_keys = jax.random.split(jax.random.key(seed), 5)
    return {
        "traces": gaussian(arg_keys[0], (SHOTS, NR, NT), 1.0, 6.0, ((0, 8), (1, 16))),
        "phases": set_ends(jax.random.randint(arg_keys[1], (SHOTS, E), 0, 64), jax.random.fold_in(arg_keys[1], 1), 0, 63).astype(jnp.int32),
        "bins": set_ends(jax.random.randint(arg_keys[2], (F,), 1, NT // 2), jax.random.fold_in(arg_keys[2], 1), 1, (NT // 2) - 1).astype(jnp.int32),
        "observed": gaussian(arg_keys[3], (E, 2, NR, F), 1.0, 6.0, ((0, 8), (2, 16)), jnp.float32),
    }


def angle_tables(bins, time_index, samples):
    phase_grid = time_index[:, None] * bins[None, :] % samples
    angle_grid = phase_grid.astype(jnp.float32) * (2.0 * math.pi / samples)
    return (jnp.cos(angle_grid), jnp.sin(angle_grid))

def reference(traces, phases, bins, observed):
    cos_table, sin_table = angle_tables(bins, jnp.arange(NT, dtype=jnp.int32), NT)
    forward_table = jnp.concatenate([cos_table, -sin_table], axis=1).astype(jnp.bfloat16)
    spectrum = jnp.dot(traces.reshape(SHOTS * NR, NT), forward_table, preferred_element_type=jnp.float32)
    spectrum = (spectrum * (1.0 / math.sqrt(NT))).reshape(SHOTS, NR, 2, F)
    code_angle = phases.astype(jnp.float32) * (2.0 * math.pi / 64.0)
    code_cos = jnp.cos(code_angle) / math.sqrt(SHOTS)
    code_sin = jnp.sin(code_angle) / math.sqrt(SHOTS)
    high = lax.Precision.HIGHEST
    spec_real = spectrum[:, :, 0, :]
    spec_imag = spectrum[:, :, 1, :]
    real_part = jnp.einsum('se,srf->erf', code_cos, spec_real, precision=high) - jnp.einsum('se,srf->erf', code_sin, spec_imag, precision=high)
    imag_part = jnp.einsum('se,srf->erf', code_sin, spec_real, precision=high) + jnp.einsum('se,srf->erf', code_cos, spec_imag, precision=high)
    encoded = jnp.stack([real_part, imag_part], axis=1)
    residual = encoded - observed
    inverse = jnp.stack([cos_table.T, -sin_table.T], axis=0) * (1.0 / math.sqrt(2 * F))
    return jnp.einsum('ecrf,cft->ert', residual, inverse, precision=high)
```

```python
import functools
import math

import jax
import jax.numpy as jnp
from jax import lax
from jax.experimental import pallas as pl
from jax.experimental.pallas import tpu as pltpu
from jax.sharding import PartitionSpec as P

MESH = pl.DeviceIdType.MESH
F32 = jnp.float32
BF16 = jnp.bfloat16

NT = 2048
NF = 256
SL = 64
RL = 64
NE = 64
G = 16
CH = 8
NCH = RL // CH
ET = 8
NX = 4
NY = 4


def trig(k):
    q = lax.shift_right_logical(k + 256, 9)
    x = (k - q * 512).astype(F32) * (2.0 * math.pi / NT)
    q = q & 3
    x2 = x * x
    s = x + x * x2 * (-1.0 / 6 + x2 * (1.0 / 120 + x2 * (-1.0 / 5040 + x2 * (1.0 / 362880))))
    c = 1.0 + x2 * (-0.5 + x2 * (1.0 / 24 + x2 * (-1.0 / 720 + x2 * (1.0 / 40320 - x2 * (1.0 / 3628800)))))
    odd = (q & 1) == 1
    cos = jnp.where(odd, s, c)
    sin = jnp.where(odd, c, s)
    cos = jnp.where((q == 1) | (q == 2), -cos, cos)
    sin = jnp.where(q >= 2, -sin, sin)
    return cos, sin


def split(v):
    hi = v.astype(BF16)
    lo = (v - hi.astype(F32)).astype(BF16)
    return hi, lo


def kernel(
    traces, phases, bins, observed, out,
    tr, ft, code, spec, part, y1a, y1b, y2l, y2r, zrv, res, zhrv, thi, tlo, obuf, base, obs,
    tr_sem, obs_sem, own_sem, y1s, y1r, y2s, y2rs, zs, zr, zhs, zhr, xs, xr,
):
    shot = lax.axis_index("shot")
    rcv = lax.axis_index("rcv")
    y = shot % 4
    zl = shot // 4
    x = rcv // 4
    zh = (rcv // 2) % 2
    core = rcv % 2

    def at_y(d):
        return {"shot": zl * 4 + (y + d + 4) % 4, "rcv": rcv}

    left, right = at_y(-1), at_y(1)
    pair = {"shot": (1 - zl) * 4 + y, "rcv": rcv}
    far = {"shot": shot, "rcv": x * 4 + (1 - zh) * 2 + core}

    def owner(dx, dc):
        xx, cc = (x + dx) % 4, (core + dc) % 2
        return xx, cc, {"shot": shot, "rcv": xx * 4 + zh * 2 + cc}

    others = [(dx, dc) for dx in (2, 1, 3, 0) for dc in (0, 1) if (dx, dc) != (0, 0)]

    barrier = pltpu.get_barrier_semaphore()
    partners = [left, right, pair, far] + [owner(dx, dc)[2] for dx, dc in others]
    for d in partners:
        pl.semaphore_signal(barrier, inc=1, device_id=d, device_id_type=MESH)

    def load(g):
        return pltpu.make_async_copy(traces.at[:, pl.ds(g * G, G), :], tr.at[g], tr_sem.at[g])

    def load_observed(h):
        return pltpu.make_async_copy(
            observed.at[:, pl.ds(h * 128, 128)], obs.at[h], obs_sem.at[h]
        )

    for g in range(RL // G):
        load(g).start()
    for h in range(2):
        load_observed(h).start()

    cc, cs = trig(phases[...] * 32)
    cc, cs = cc * (1.0 / 1024), cs * (1.0 / 1024)
    mat = jnp.concatenate(
        [jnp.concatenate([cc, cs], axis=1), jnp.concatenate([-cs, cc], axis=1)], axis=0
    ).T
    rows = []
    for yy in range(NY):
        for zz in range(2):
            for c in range(2):
                at = c * NE + zz * 32 + yy * 8
                rows.append(mat[at : at + 8, :])
    mat = jnp.concatenate(rows, axis=0)
    chi, clo = split(mat)
    code[...] = jnp.concatenate(
        [jnp.concatenate([chi, chi], axis=1), jnp.concatenate([clo, clo], axis=1)], axis=0
    )

    row = lax.broadcasted_iota(jnp.int32, (128, NF), 0)
    b = jnp.broadcast_to(bins[...], (128, NF))
    cosb, sinb = trig((row * b) & (NT - 1))
    base[0] = cosb
    base[1] = sinb
    row16 = lax.broadcasted_iota(jnp.int32, (16, NF), 0)
    cosa, sina = trig((row16 * 128 * b[:16]) & (NT - 1))
    base[2, 0:16] = cosa
    base[3, 0:16] = sina

    def forward_rows(a, _):
        ca, sa = base[2, pl.ds(a, 1), :], base[3, pl.ds(a, 1), :]
        cb, sb = base[0], base[1]
        at = pl.ds(pl.multiple_of(a * 128, 128), 128)
        ft[at, 0:NF] = (ca * cb - sa * sb).astype(BF16)
        ft[at, NF : 2 * NF] = (-(sa * cb + ca * sb)).astype(BF16)
        return 0

    lax.fori_loop(0, 16, forward_rows, 0)

    def inverse_table():
        scale = 1.0 / math.sqrt(2 * NF)
        blk = lax.broadcasted_iota(jnp.int32, (128, NF), 0)
        blk = ((blk // 2) * 4 + zh * 2 + blk % 2) & 15
        ca, sa = trig((blk * 128 * b) & (NT - 1))
        ca, sa = (ca * scale).T, (sa * scale).T
        cb, sb = base[0].T, base[1].T
        for i in range(2 * NX):
            ci, si = ca[:, i : i + 1], sa[:, i : i + 1]
            cols = slice(i * 128, (i + 1) * 128)
            hi, lo = split(ci * cb - si * sb)
            thi[0:NF, cols] = hi
            tlo[0:NF, cols] = lo
            hi, lo = split(-(si * cb + ci * sb))
            thi[NF : 2 * NF, cols] = hi
            tlo[NF : 2 * NF, cols] = lo

    def remote(src, dst, send, recv, device):
        return pltpu.make_async_remote_copy(
            src_ref=src, dst_ref=dst, send_sem=send, recv_sem=recv, device_id=device, device_id_type=MESH
        )

    opp, nxt, prv = (y + 2) % 4, (y + 1) % 4, (y + 3) % 4

    def copy(name, i):
        r = pl.ds(i * CH, CH)
        table = {
            "a1": (part.at[opp, 0, :, r], y1a.at[:, r], y1s.at[0, i], y1r.at[0, i], right),
            "b1": (part.at[opp, 1, :, r], y1b.at[:, r], y1s.at[1, i], y1r.at[1, i], left),
            "l1": (part.at[nxt, 1, :, r], y2l.at[1, :, r], y2s.at[0, i], y2rs.at[0, i], right),
            "r0": (part.at[prv, 0, :, r], y2r.at[0, :, r], y2s.at[1, i], y2rs.at[1, i], left),
            "l0": (part.at[nxt, 0, :, r], y2l.at[0, :, r], y2s.at[2, i], y2rs.at[2, i], right),
            "r1": (part.at[prv, 1, :, r], y2r.at[1, :, r], y2s.at[3, i], y2rs.at[3, i], left),
            "z": (part.at[y, 1 - zl, :, r], zrv.at[:, r], zs.at[i], zr.at[i], pair),
            "h": (res.at[:, r], zhrv.at[:, r], zhs.at[i], zhr.at[i], far),
        }
        return remote(*table[name])

    def forward(g):
        load(g).wait()

        def tile(m, _):
            xs_ = tr[g, pl.ds(m * 16, 16)].reshape(16 * G, NT)
            v = jnp.dot(xs_, ft[...], preferred_element_type=F32)
            for q in range(4):
                spec[q, pl.ds(pl.multiple_of(m * 16 * G, 16 * G), 16 * G), :] = v[
                    :, q * 128 : (q + 1) * 128
                ]
            return 0

        lax.fori_loop(0, SL // 16, tile, 0)

    def encode(i):
        for j in range(CH):
            at = pl.ds((i % 2) * CH + j, SL, stride=G)
            re = jnp.concatenate([spec[0, at, :], spec[1, at, :]], axis=1)
            im = jnp.concatenate([spec[2, at, :], spec[3, at, :]], axis=1)
            hi, lo = split(jnp.concatenate([re, im], axis=0))
            both = jnp.dot(
                code[...], jnp.concatenate([hi, lo], axis=0), preferred_element_type=F32
            )
            part[:, :, :, i * CH + j] = (both[0:128] + both[128:256]).reshape(NY, 2, 2, ET, NF)

    def inverse(src, i, which):
        r = pl.ds(i * CH, CH)
        v = jnp.concatenate(
            [src[0, r].reshape(CH * ET, NF), src[1, r].reshape(CH * ET, NF)], axis=1
        )
        hi, lo = split(v)
        hl = jnp.concatenate([hi, lo], axis=0)
        n = CH * ET
        for xx in range(NX):
            cols = slice(xx * 256, (xx + 1) * 256)
            both = jnp.dot(hl, thi[:, cols], preferred_element_type=F32)
            o = both[0:n] + both[n : 2 * n] + jnp.dot(hi, tlo[:, cols], preferred_element_type=F32)
            for c in range(2):
                obuf[xx, c, pl.ds(which * RL + i * CH, CH)] = o[:, c * 128 : (c + 1) * 128].reshape(
                    CH, ET, 128
                )
        from_rcv = x * 4 + core + 2 * (zh if which == 0 else 1 - zh)
        dst = out.at[pl.ds(from_rcv * RL + i * CH, CH)]
        rows_ = pl.ds(which * RL + i * CH, CH)
        for dx, dc in others:
            xx, c, device = owner(dx, dc)
            remote(
                obuf.at[xx, c, rows_], dst, xs.at[xx * 2 + c], xr.at[x * 2 + core], device
            ).start()
        pltpu.make_async_copy(obuf.at[x, core, rows_], dst, own_sem).start()

    def step(i, _):
        @pl.when(i < NCH)
        def _():
            @pl.when(i % 2 == 0)
            def _():
                forward(i // 2)

            encode(i)

        @pl.when(i == 0)
        def _():
            pl.semaphore_wait(barrier, len(partners))

        @pl.when(i < NCH)
        def _():
            for k in ("a1", "b1", "l1", "r0"):
                copy(k, i).start()

        @pl.when(i == 0)
        def _():
            inverse_table()
            for h in range(2):
                load_observed(h).wait()

        @pl.when((i >= 1) & (i < NCH + 1))
        def _():
            k = i - 1
            r = pl.ds(k * CH, CH)
            copy("a1", k).wait_recv()
            part[nxt, 0, :, r] = part[nxt, 0, :, r] + y1a[:, r]
            copy("l0", k).start()
            copy("b1", k).wait_recv()
            part[prv, 1, :, r] = part[prv, 1, :, r] + y1b[:, r]
            copy("r1", k).start()

        @pl.when((i >= 2) & (i < NCH + 2))
        def _():
            k = i - 2
            r = pl.ds(k * CH, CH)
            for name in ("l1", "r0", "l0", "r1"):
                copy(name, k).wait_recv()
            part[y, 1 - zl, :, r] = part[y, 1 - zl, :, r] + y2l[1 - zl, :, r] + y2r[1 - zl, :, r]
            copy("z", k).start()
            res[:, r] = part[y, zl, :, r] + y2l[zl, :, r] + y2r[zl, :, r]
            for p in range(2):
                for j in range(CH):
                    at = k * CH + j
                    rows = pl.ds(p * RL + at, ET, stride=2 * RL)
                    seen = jnp.concatenate([obs[0, rows, :], obs[1, rows, :]], axis=1)
                    res[p, at] = res[p, at] - seen

        @pl.when((i >= 3) & (i < NCH + 3))
        def _():
            k = i - 3
            r = pl.ds(k * CH, CH)
            copy("z", k).wait_recv()
            res[:, r] = res[:, r] + zrv[:, r]
            copy("h", k).start()
            inverse(res, k, 0)

        @pl.when(i >= 4)
        def _():
            k = i - 4
            copy("h", k).wait_recv()
            inverse(zhrv, k, 1)

        return 0

    lax.fori_loop(0, NCH + 4, step, 0)

    def drain(i, _):
        for name in ("a1", "b1", "l1", "r0", "l0", "r1", "z", "h"):
            copy(name, i).wait_send()
        return 0

    lax.fori_loop(0, NCH, drain, 0)
    whole = out.at[pl.ds(0, 2 * RL)]
    pltpu.make_async_copy(obuf.at[x, core], whole, own_sem).wait()
    for dx, dc in others:
        xx, c, device = owner(dx, dc)
        both = remote(obuf.at[xx, c], whole, xs.at[xx * 2 + c], xr.at[xx * 2 + c], device)
        both.wait_send()
        both.wait_recv()


def body(traces, phases, bins, observed):
    dma = pltpu.SemaphoreType.DMA
    vmem = lambda *s: pltpu.VMEM(s, F32)
    whole = pl.BlockSpec(memory_space=pltpu.VMEM)
    anywhere = pl.BlockSpec(memory_space=pl.ANY)
    flops = 2 * (SL * RL * NT * 2 * NF + 4 * 128 * 128 * RL * NF + 3 * 1024 * 512 * 1024)
    rows = pl.pallas_call(
        kernel,
        out_shape=jax.ShapeDtypeStruct((16 * RL, ET, 128), F32),
        in_specs=[anywhere, whole, whole, anywhere],
        out_specs=anywhere,
        scratch_shapes=[
            pltpu.VMEM((RL // G, SL, G, NT), BF16),
            pltpu.VMEM((NT, 2 * NF), BF16),
            pltpu.VMEM((256, 256), BF16),
            vmem(4, SL * G, 128),
            vmem(NY, 2, 2, RL, ET, NF),
            vmem(2, RL, ET, NF),
            vmem(2, RL, ET, NF),
            vmem(2, 2, RL, ET, NF),
            vmem(2, 2, RL, ET, NF),
            vmem(2, RL, ET, NF),
            vmem(2, RL, ET, NF),
            vmem(2, RL, ET, NF),
            pltpu.VMEM((2 * NF, 1024), BF16),
            pltpu.VMEM((2 * NF, 1024), BF16),
            vmem(NX, 2, 2 * RL, ET, 128),
            vmem(4, 128, NF),
            vmem(2, ET * 2 * RL, 128),
            dma((RL // G,)),
            dma((2,)),
            dma,
            dma((2, NCH)),
            dma((2, NCH)),
            dma((4, NCH)),
            dma((4, NCH)),
            dma((NCH,)),
            dma((NCH,)),
            dma((NCH,)),
            dma((NCH,)),
            dma((8,)),
            dma((8,)),
        ],
        compiler_params=pltpu.CompilerParams(
            collective_id=0, has_side_effects=True, vmem_limit_bytes=58 * 2**20
        ),
        cost_estimate=pl.CostEstimate(flops=flops, bytes_accessed=22 * 2**20, transcendentals=0),
    )(traces, phases, bins.reshape(1, NF), observed.reshape(ET * 2 * RL, NF))
    return rows.transpose(1, 0, 2)


def solution(mesh):
    in_specs = (P("shot", "rcv", None), P("shot", None), P(), P("shot", None, "rcv", None))
    out_specs = P("shot", None, "rcv")
    return jax.shard_map(body, mesh=mesh, in_specs=in_specs, out_specs=out_specs, check_vma=False)
```

```python
import functools
import math

import jax
import jax.numpy as jnp
from jax import lax
from jax.experimental import pallas as pl
from jax.experimental.pallas import tpu as pltpu
from jax.sharding import PartitionSpec as P

MESH = pl.DeviceIdType.MESH
F32 = jnp.float32
BF16 = jnp.bfloat16

NT = 2048
NF = 256
SL = 64
RL = 64
NE = 64
G = 16
CH = 4
NCH = RL // CH
ZS = (12, 13, 15)
SEQ = (0, 1, 2, 3, 4, 5, 6, 7, 12, 13, 8, 9, 10, 11, 14, 15)
PG = G // CH
LAST = RL // G - 1
LAGS = ((2, ()), (4, ()), (6, (13,)), (8, (12, 14)))
ZG = 1
ZAT = (1, 3, 8)
ET = 8
NX = 4
NY = 4


def trig(k):
    q = lax.shift_right_logical(k + 256, 9)
    x = (k - q * 512).astype(F32) * (2.0 * math.pi / NT)
    q = q & 3
    x2 = x * x
    s = x + x * x2 * (-1.0 / 6 + x2 * (1.0 / 120 + x2 * (-1.0 / 5040 + x2 * (1.0 / 362880))))
    c = 1.0 + x2 * (-0.5 + x2 * (1.0 / 24 + x2 * (-1.0 / 720 + x2 * (1.0 / 40320 - x2 * (1.0 / 3628800)))))
    odd = (q & 1) == 1
    cos = jnp.where(odd, s, c)
    sin = jnp.where(odd, c, s)
    cos = jnp.where((q == 1) | (q == 2), -cos, cos)
    sin = jnp.where(q >= 2, -sin, sin)
    return cos, sin


def split(v):
    hi = v.astype(BF16)
    lo = (v - hi.astype(F32)).astype(BF16)
    return hi, lo


def kernel(
    traces, phases, bins, observed, out,
    tr, ft, code, spec, part, y1a, y1b, y2l, y2r, zrv, zzrv, res, zhrv, thi, tlo, obuf, base, obs,
    ph, bn, tr_sem, obs_sem, in_sem, own_sem, y1s, y1r, y2s, y2rs, zs, zr, zhs, zhr, xs, xr,
):
    shot = lax.axis_index("shot")
    rcv = lax.axis_index("rcv")
    y = shot % 4
    zl = shot // 4
    x = rcv // 4
    zh = (rcv // 2) % 2
    core = rcv % 2

    def at_y(d):
        return {"shot": zl * 4 + (y + d + 4) % 4, "rcv": rcv}

    left, right = at_y(-1), at_y(1)
    pair = {"shot": (1 - zl) * 4 + y, "rcv": rcv}
    far = {"shot": shot, "rcv": x * 4 + (1 - zh) * 2 + core}

    def owner(dx, dc):
        xx, cc = (x + dx) % 4, (core + dc) % 2
        return xx, cc, {"shot": shot, "rcv": xx * 4 + zh * 2 + cc}

    others = [(dx, dc) for dx in (2, 1, 3, 0) for dc in (0, 1) if (dx, dc) != (0, 0)]

    barrier = pltpu.get_barrier_semaphore()
    partners = [left, right, pair, far] + [owner(dx, dc)[2] for dx, dc in others]
    for d in partners:
        pl.semaphore_signal(barrier, inc=1, device_id=d, device_id_type=MESH)

    def load(g):
        return pltpu.make_async_copy(traces.at[:, pl.ds(g * G, G), :], tr.at[g], tr_sem.at[g])

    def load_observed(h):
        return pltpu.make_async_copy(
            observed.at[:, pl.ds(h * 128, 128)], obs.at[h], obs_sem.at[h]
        )

    load_phases = pltpu.make_async_copy(phases, ph, in_sem.at[0])
    load_bins = pltpu.make_async_copy(bins, bn, in_sem.at[1])
    load_bins.start()
    load_phases.start()
    for g in (0, LAST, *range(1, LAST)):
        load(g).start()
    for h in range(2):
        load_observed(h).start()

    load_phases.wait()
    cc, cs = trig(ph[...] * 32)
    cc, cs = cc * (1.0 / 1024), cs * (1.0 / 1024)
    mat = jnp.concatenate(
        [jnp.concatenate([cc, cs], axis=1), jnp.concatenate([-cs, cc], axis=1)], axis=0
    ).T
    rows = []
    for yy in range(NY):
        for zz in range(2):
            for c in range(2):
                at = c * NE + zz * 32 + yy * 8
                rows.append(mat[at : at + 8, :])
    mat = jnp.concatenate(rows, axis=0)
    chi, clo = split(mat)
    code[...] = jnp.concatenate(
        [jnp.concatenate([chi, chi], axis=1), jnp.concatenate([clo, clo], axis=1)], axis=0
    )

    row = lax.broadcasted_iota(jnp.int32, (128, NF), 0)
    load_bins.wait()
    b = jnp.broadcast_to(bn[...], (128, NF))
    cosb, sinb = trig((row * b) & (NT - 1))
    base[0] = cosb
    base[1] = sinb
    row16 = lax.broadcasted_iota(jnp.int32, (16, NF), 0)
    cosa, sina = trig((row16 * 128 * b[:16]) & (NT - 1))
    base[2, 0:16] = cosa
    base[3, 0:16] = sina

    def forward_rows(a, _):
        ca, sa = base[2, pl.ds(a, 1), :], base[3, pl.ds(a, 1), :]
        cb, sb = base[0], base[1]
        at = pl.ds(pl.multiple_of(a * 128, 128), 128)
        ft[at, 0:NF] = (ca * cb - sa * sb).astype(BF16)
        ft[at, NF : 2 * NF] = (-(sa * cb + ca * sb)).astype(BF16)
        return 0

    lax.fori_loop(0, 16, forward_rows, 0)

    def inverse_table():
        scale = 1.0 / math.sqrt(2 * NF)
        blk = lax.broadcasted_iota(jnp.int32, (128, NF), 0)
        blk = ((blk // 2) * 4 + zh * 2 + blk % 2) & 15
        ca, sa = trig((blk * 128 * b) & (NT - 1))
        ca, sa = (ca * scale).T, (sa * scale).T
        cb, sb = base[0].T, base[1].T
        for i in range(2 * NX):
            ci, si = ca[:, i : i + 1], sa[:, i : i + 1]
            cols = slice(i * 128, (i + 1) * 128)
            hi, lo = split(ci * cb - si * sb)
            thi[0:NF, cols] = hi
            tlo[0:NF, cols] = lo
            hi, lo = split(-(si * cb + ci * sb))
            thi[NF : 2 * NF, cols] = hi
            tlo[NF : 2 * NF, cols] = lo

    def remote(src, dst, send, recv, device):
        return pltpu.make_async_remote_copy(
            src_ref=src, dst_ref=dst, send_sem=send, recv_sem=recv, device_id=device, device_id_type=MESH
        )

    opp, nxt, prv = (y + 2) % 4, (y + 1) % 4, (y + 3) % 4

    def copy(name, i):
        r = pl.ds(i * CH, CH)
        table = {
            "a1": (part.at[opp, 0, :, r], y1a.at[:, r], y1s.at[0, i], y1r.at[0, i], right),
            "b1": (part.at[opp, 1, :, r], y1b.at[:, r], y1s.at[1, i], y1r.at[1, i], left),
            "l1": (part.at[nxt, 1, :, r], y2l.at[1, :, r], y2s.at[0, i], y2rs.at[0, i], right),
            "r0": (part.at[prv, 0, :, r], y2r.at[0, :, r], y2s.at[1, i], y2rs.at[1, i], left),
            "l0": (part.at[nxt, 0, :, r], y2l.at[0, :, r], y2s.at[2, i], y2rs.at[2, i], right),
            "r1": (part.at[prv, 1, :, r], y2r.at[1, :, r], y2s.at[3, i], y2rs.at[3, i], left),
            "z": (part.at[y, 1 - zl, :, r], zrv.at[:, r], zs.at[i], zr.at[i], pair),
            "h": (res.at[:, r], zhrv.at[:, r], zhs.at[i], zhr.at[i], far),
        }
        return remote(*table[name])

    def zcopy(name, i):
        r = pl.ds(i * CH, CH)
        rz = pl.ds((i - LAST * PG) * CH, CH)
        table = {
            "zz": (part.at[:, 1 - zl, :, r], zzrv.at[:, :, rz], zs.at[i], zr.at[i], pair),
            "a1": (part.at[opp, zl, 0, r], y1a.at[0, r], y1s.at[0, i], y1r.at[0, i], right),
            "b1": (part.at[opp, zl, 1, r], y1b.at[0, r], y1s.at[1, i], y1r.at[1, i], left),
            "l1": (part.at[nxt, zl, 1, r], y2l.at[0, 1, r], y2s.at[0, i], y2rs.at[0, i], right),
            "r0": (part.at[prv, zl, 0, r], y2r.at[0, 0, r], y2s.at[1, i], y2rs.at[1, i], left),
            "l0": (part.at[nxt, zl, 0, r], y2l.at[0, 0, r], y2s.at[2, i], y2rs.at[2, i], right),
            "r1": (part.at[prv, zl, 1, r], y2r.at[0, 1, r], y2s.at[3, i], y2rs.at[3, i], left),
        }
        return remote(*table[name])

    def forward(g):
        load(g).wait()

        def tile(m, _):
            xs_ = tr[g, pl.ds(m * 16, 16)].reshape(16 * G, NT)
            v = jnp.dot(xs_, ft[...], preferred_element_type=F32)
            for q in range(4):
                spec[q, pl.ds(pl.multiple_of(m * 16 * G, 16 * G), 16 * G), :] = v[
                    :, q * 128 : (q + 1) * 128
                ]
            return 0

        lax.fori_loop(0, SL // 16, tile, 0)

    def encode(i):
        for j in range(CH):
            at = pl.ds((i % PG) * CH + j, SL, stride=G)
            re = jnp.concatenate([spec[0, at, :], spec[1, at, :]], axis=1)
            im = jnp.concatenate([spec[2, at, :], spec[3, at, :]], axis=1)
            hi, lo = split(jnp.concatenate([re, im], axis=0))
            both = jnp.dot(
                code[...], jnp.concatenate([hi, lo], axis=0), preferred_element_type=F32
            )
            part[:, :, :, i * CH + j] = (both[0:128] + both[128:256]).reshape(NY, 2, 2, ET, NF)

    def inverse(src, i, which):
        r = pl.ds(i * CH, CH)
        v = jnp.concatenate(
            [src[0, r].reshape(CH * ET, NF), src[1, r].reshape(CH * ET, NF)], axis=1
        )
        hi, lo = split(v)
        hl = jnp.concatenate([hi, lo], axis=0)
        n = CH * ET
        for xx in range(NX):
            cols = slice(xx * 256, (xx + 1) * 256)
            both = jnp.dot(hl, thi[:, cols], preferred_element_type=F32)
            o = both[0:n] + both[n : 2 * n] + jnp.dot(hi, tlo[:, cols], preferred_element_type=F32)
            for c in range(2):
                obuf[xx, c, pl.ds(which * RL + i * CH, CH)] = o[:, c * 128 : (c + 1) * 128].reshape(
                    CH, ET, 128
                )
        from_rcv = x * 4 + core + 2 * (zh if which == 0 else 1 - zh)
        dst = out.at[pl.ds(from_rcv * RL + i * CH, CH)]
        rows_ = pl.ds(which * RL + i * CH, CH)
        for dx, dc in others:
            xx, c, device = owner(dx, dc)
            remote(
                obuf.at[xx, c, rows_], dst, xs.at[xx * 2 + c], xr.at[x * 2 + core], device
            ).start()
        pltpu.make_async_copy(obuf.at[x, core, rows_], dst, own_sem).start()

    def less_observed(k):
        for p in range(2):
            for j in range(CH):
                at = k * CH + j
                rows = pl.ds(p * RL + at, ET, stride=2 * RL)
                seen = jnp.concatenate([obs[0, rows, :], obs[1, rows, :]], axis=1)
                res[p, at] = res[p, at] - seen

    def done(i, lag, earlier):
        n = i - lag + 1
        for at in earlier:
            n = n + jnp.where(i >= at, 1, 0)
        return jnp.clip(n, 0, NCH)

    def chunk(p):
        c = p
        for at in range(1, NCH):
            jump = SEQ[at] - SEQ[at - 1] - 1
            if jump:
                c = c + jnp.where(p >= at, jump, 0)
        return c

    def early(c):
        hit = c == ZS[0]
        for other in ZS[1:]:
            hit = hit | (c == other)
        return hit

    def stage0(p):
        c = chunk(p)
        z = early(c)

        @pl.when(c < LAST * PG)
        def _():
            @pl.when(c % PG == 0)
            def _():
                forward(c // PG)
                encode(c)

            @pl.when(c % PG == 1)
            def _():
                lax.fori_loop(c, c + PG - 1, lambda k, _: (encode(k), 0)[1], 0)

        @pl.when(p == 0)
        def _():
            pl.semaphore_wait(barrier, len(partners))

        @pl.when(jnp.logical_not(z))
        def _():
            for name in ("a1", "b1", "l1", "r0"):
                copy(name, c).start()

        @pl.when(z)
        def _():
            zcopy("zz", c).wait_recv()
            r = pl.ds(c * CH, CH)
            part[:, zl, :, r] = part[:, zl, :, r] + zzrv[:, :, pl.ds((c - LAST * PG) * CH, CH)]
            for name in ("a1", "b1", "l1", "r0"):
                zcopy(name, c).start()

    def stage1(p, _):
        c = chunk(p)
        z = early(c)
        r = pl.ds(c * CH, CH)

        @pl.when(jnp.logical_not(z))
        def _():
            copy("a1", c).wait_recv()
            part[nxt, 0, :, r] = part[nxt, 0, :, r] + y1a[:, r]
            copy("l0", c).start()
            copy("b1", c).wait_recv()
            part[prv, 1, :, r] = part[prv, 1, :, r] + y1b[:, r]
            copy("r1", c).start()

        @pl.when(z)
        def _():
            zcopy("a1", c).wait_recv()
            part[nxt, zl, 0, r] = part[nxt, zl, 0, r] + y1a[0, r]
            zcopy("l0", c).start()
            zcopy("b1", c).wait_recv()
            part[prv, zl, 1, r] = part[prv, zl, 1, r] + y1b[0, r]
            zcopy("r1", c).start()

        return 0

    def stage2(p, _):
        c = chunk(p)
        z = early(c)
        r = pl.ds(c * CH, CH)

        @pl.when(jnp.logical_not(z))
        def _():
            for name in ("l1", "r0", "l0", "r1"):
                copy(name, c).wait_recv()
            part[y, 1 - zl, :, r] = part[y, 1 - zl, :, r] + y2l[1 - zl, :, r] + y2r[1 - zl, :, r]
            copy("z", c).start()
            res[:, r] = part[y, zl, :, r] + y2l[zl, :, r] + y2r[zl, :, r]
            less_observed(c)

        @pl.when(z)
        def _():
            for name in ("l1", "r0", "l0", "r1"):
                zcopy(name, c).wait_recv()
            res[:, r] = part[y, zl, :, r] + y2l[0, :, r] + y2r[0, :, r]
            less_observed(c)
            copy("h", c).start()
            inverse(res, c, 0)

        return 0

    def stage3(p, _):
        c = chunk(p)

        @pl.when(jnp.logical_not(early(c)))
        def _():
            r = pl.ds(c * CH, CH)
            copy("z", c).wait_recv()
            res[:, r] = res[:, r] + zrv[:, r]
            copy("h", c).start()
            inverse(res, c, 0)

        return 0

    def stage4(p, _):
        c = chunk(p)
        copy("h", c).wait_recv()
        inverse(zhrv, c, 1)
        return 0

    def step(i, _):
        @pl.when(i < NCH)
        def _():
            stage0(i)

        @pl.when(i == 2)
        def _():
            inverse_table()
            for h in range(2):
                load_observed(h).wait()

        @pl.when(i == ZG)
        def _():
            forward(LAST)
            lax.fori_loop(LAST * PG, NCH, lambda k, _: (encode(k), 0)[1], 0)

        for at, c in zip(ZAT, ZS):
            @pl.when(i == at)
            def _(c=c):
                zcopy("zz", c).start()

        for stage, (lag, earlier) in zip((stage1, stage2, stage3, stage4), LAGS):
            lax.fori_loop(done(i - 1, lag, earlier), done(i, lag, earlier), stage, 0)
        return 0

    lax.fori_loop(0, NCH + LAGS[3][0] - len(LAGS[3][1]), step, 0)

    def drain(c, _):
        z = early(c)

        @pl.when(jnp.logical_not(z))
        def _():
            for name in ("a1", "b1", "l1", "r0", "l0", "r1", "z"):
                copy(name, c).wait_send()

        @pl.when(z)
        def _():
            for name in ("a1", "b1", "l1", "r0", "l0", "r1", "zz"):
                zcopy(name, c).wait_send()

        copy("h", c).wait_send()
        return 0

    lax.fori_loop(0, NCH, drain, 0)
    whole = out.at[pl.ds(0, 2 * RL)]
    pltpu.make_async_copy(obuf.at[x, core], whole, own_sem).wait()
    for dx, dc in others:
        xx, c, device = owner(dx, dc)
        both = remote(obuf.at[xx, c], whole, xs.at[xx * 2 + c], xr.at[xx * 2 + c], device)
        both.wait_send()
        both.wait_recv()


def body(traces, phases, bins, observed):
    dma = pltpu.SemaphoreType.DMA
    vmem = lambda *s: pltpu.VMEM(s, F32)
    hbm = pl.BlockSpec(memory_space=pltpu.HBM)
    flops = 2 * (SL * RL * NT * 2 * NF + 4 * 128 * 128 * RL * NF + 3 * 1024 * 512 * 1024)
    arrays = (traces, phases, bins.reshape(1, NF), observed.reshape(ET * 2 * RL, NF))
    rows = pl.pallas_call(
        kernel,
        out_shape=pltpu.VMEM((16 * RL, ET, 128), F32),
        in_specs=[hbm, hbm, hbm, hbm],
        out_specs=pl.BlockSpec(memory_space=pl.ANY),
        scratch_shapes=[
            pltpu.VMEM((RL // G, SL, G, NT), BF16),
            pltpu.VMEM((NT, 2 * NF), BF16),
            pltpu.VMEM((256, 256), BF16),
            vmem(4, SL * G, 128),
            vmem(NY, 2, 2, RL, ET, NF),
            vmem(2, RL, ET, NF),
            vmem(2, RL, ET, NF),
            vmem(2, 2, RL, ET, NF),
            vmem(2, 2, RL, ET, NF),
            vmem(2, RL, ET, NF),
            vmem(NY, 2, G, ET, NF),
            vmem(2, RL, ET, NF),
            vmem(2, RL, ET, NF),
            pltpu.VMEM((2 * NF, 1024), BF16),
            pltpu.VMEM((2 * NF, 1024), BF16),
            vmem(NX, 2, 2 * RL, ET, 128),
            vmem(4, 128, NF),
            vmem(2, ET * 2 * RL, 128),
            pltpu.VMEM((SL, NE), jnp.int32),
            pltpu.VMEM((1, NF), jnp.int32),
            dma((RL // G,)),
            dma((2,)),
            dma((2,)),
            dma,
            dma((2, NCH)),
            dma((2, NCH)),
            dma((4, NCH)),
            dma((4, NCH)),
            dma((NCH,)),
            dma((NCH,)),
            dma((NCH,)),
            dma((NCH,)),
            dma((8,)),
            dma((8,)),
        ],
        compiler_params=pltpu.CompilerParams(
            collective_id=0, has_side_effects=True, vmem_limit_bytes=49 * 2**20
        ),
        cost_estimate=pl.CostEstimate(flops=flops, bytes_accessed=22 * 2**20, transcendentals=0),
    )(*(pltpu.with_memory_space_constraint(a, pltpu.HBM) for a in arrays))
    return rows.transpose(1, 0, 2)


def solution(mesh):
    in_specs = (P("shot", "rcv", None), P("shot", None), P(), P("shot", None, "rcv", None))
    out_specs = P("shot", None, "rcv")
    return jax.shard_map(body, mesh=mesh, in_specs=in_specs, out_specs=out_specs, check_vma=False)
```

```python
import functools
import math

import jax
import jax.numpy as jnp
from jax import lax
from jax.experimental import pallas as pl
from jax.experimental.pallas import tpu as pltpu
from jax.sharding import PartitionSpec as P

MESH = pl.DeviceIdType.MESH
F32 = jnp.float32
BF16 = jnp.bfloat16

NT = 2048
NF = 256
SL = 64
RL = 64
NE = 64
G = 16
CH = 4
NCH = RL // CH
ZS = (12, 13, 14)
SEQ = (0, 1, 2, 3, 4, 5, 6, 7, 8, 12, 9, 13, 10, 14, 11, 15)
PG = G // CH
LAST = RL // G - 1
STEPS = (
    (1, 4, 4, 4, 4, 6, 7, 8, 9, 11, 12, 13, 14, 18, 18, 21),
    (3, 4, 5, 6, 6, 8, 10, 11, 12, 13, 15, 17, 20, 21, 22, 23),
    (5, 5, 8, 8, 9, 11, 11, 13, 13, 16, 17, 17, 21, 22, 24, 25),
    (6, 7, 8, 10, 10, 12, 12, 13, 15, 16, 20, 20, 23, 23, 24, 26),
)
ZG = 1
ZAT = (3, 7, 1)
ET = 8
NX = 4
NY = 4


def trig(k):
    q = lax.shift_right_logical(k + 256, 9)
    x = (k - q * 512).astype(F32) * (2.0 * math.pi / NT)
    q = q & 3
    x2 = x * x
    s = x + x * x2 * (-1.0 / 6 + x2 * (1.0 / 120 + x2 * (-1.0 / 5040 + x2 * (1.0 / 362880))))
    c = 1.0 + x2 * (-0.5 + x2 * (1.0 / 24 + x2 * (-1.0 / 720 + x2 * (1.0 / 40320 - x2 * (1.0 / 3628800)))))
    odd = (q & 1) == 1
    cos = jnp.where(odd, s, c)
    sin = jnp.where(odd, c, s)
    cos = jnp.where((q == 1) | (q == 2), -cos, cos)
    sin = jnp.where(q >= 2, -sin, sin)
    return cos, sin


def split(v):
    hi = v.astype(BF16)
    lo = (v - hi.astype(F32)).astype(BF16)
    return hi, lo


def kernel(
    traces, phases, bins, observed, out,
    tr, ft, code, spec, part, y1a, y1b, y2l, y2r, zrv, zzrv, res, zhrv, zgrv, thi, tlo, obuf, base, obs,
    ph, bn, tr_sem, obs_sem, in_sem, own_sem, y1s, y1r, y2s, y2rs, zs, zr, zhs, zhr, zgs, zgr, xs, xr,
):
    shot = lax.axis_index("shot")
    rcv = lax.axis_index("rcv")
    y = shot % 4
    zl = shot // 4
    x = rcv // 4
    zh = (rcv // 2) % 2
    core = rcv % 2

    def at_y(d):
        return {"shot": zl * 4 + (y + d + 4) % 4, "rcv": rcv}

    left, right = at_y(-1), at_y(1)
    pair = {"shot": (1 - zl) * 4 + y, "rcv": rcv}
    far = {"shot": shot, "rcv": x * 4 + (1 - zh) * 2 + core}
    cross = {"shot": (1 - zl) * 4 + y, "rcv": x * 4 + (1 - zh) * 2 + core}

    def owner(dx, dc):
        xx, cc = (x + dx) % 4, (core + dc) % 2
        return xx, cc, {"shot": shot, "rcv": xx * 4 + zh * 2 + cc}

    others = [(dx, dc) for dx in (2, 1, 3, 0) for dc in (0, 1) if (dx, dc) != (0, 0)]

    barrier = pltpu.get_barrier_semaphore()
    partners = [left, right, pair, far, cross] + [owner(dx, dc)[2] for dx, dc in others]
    for d in partners:
        pl.semaphore_signal(barrier, inc=1, device_id=d, device_id_type=MESH)

    def load(g):
        return pltpu.make_async_copy(traces.at[:, pl.ds(g * G, G), :], tr.at[g], tr_sem.at[g])

    def load_observed(h):
        return pltpu.make_async_copy(
            observed.at[:, pl.ds(h * 128, 128)], obs.at[h], obs_sem.at[h]
        )

    load_phases = pltpu.make_async_copy(phases, ph, in_sem.at[0])
    load_bins = pltpu.make_async_copy(bins, bn, in_sem.at[1])
    load_bins.start()
    load_phases.start()
    load(0).start()

    load_phases.wait()
    cc, cs = trig(ph[...] * 32)
    cc, cs = cc * (1.0 / 1024), cs * (1.0 / 1024)
    mat = jnp.concatenate(
        [jnp.concatenate([cc, cs], axis=1), jnp.concatenate([-cs, cc], axis=1)], axis=0
    ).T
    rows = []
    for yy in range(NY):
        for zz in range(2):
            for c in range(2):
                at = c * NE + zz * 32 + yy * 8
                rows.append(mat[at : at + 8, :])
    mat = jnp.concatenate(rows, axis=0)
    chi, clo = split(mat)
    code[...] = jnp.concatenate(
        [jnp.concatenate([chi, chi], axis=1), jnp.concatenate([clo, clo], axis=1)], axis=0
    )

    row = lax.broadcasted_iota(jnp.int32, (128, NF), 0)
    load_bins.wait()
    b = jnp.broadcast_to(bn[...], (128, NF))
    cosb, sinb = trig((row * b) & (NT - 1))
    base[0] = cosb
    base[1] = sinb
    row16 = lax.broadcasted_iota(jnp.int32, (16, NF), 0)
    cosa, sina = trig((row16 * 128 * b[:16]) & (NT - 1))
    base[2, 0:16] = cosa
    base[3, 0:16] = sina

    def forward_rows(a, _):
        ca, sa = base[2, pl.ds(a, 1), :], base[3, pl.ds(a, 1), :]
        cb, sb = base[0], base[1]
        at = pl.ds(pl.multiple_of(a * 128, 128), 128)
        ft[at, 0:NF] = (ca * cb - sa * sb).astype(BF16)
        ft[at, NF : 2 * NF] = (-(sa * cb + ca * sb)).astype(BF16)
        return 0

    lax.fori_loop(0, 16, forward_rows, 0)
    load(0).wait()
    for g in (LAST, *range(1, LAST)):
        load(g).start()
    for h in range(2):
        load_observed(h).start()

    def inverse_table():
        scale = 1.0 / math.sqrt(2 * NF)
        blk = lax.broadcasted_iota(jnp.int32, (128, NF), 0)
        blk = ((blk // 2) * 4 + zh * 2 + blk % 2) & 15
        ca, sa = trig((blk * 128 * b) & (NT - 1))
        ca, sa = (ca * scale).T, (sa * scale).T
        cb, sb = base[0].T, base[1].T
        for i in range(2 * NX):
            ci, si = ca[:, i : i + 1], sa[:, i : i + 1]
            cols = slice(i * 128, (i + 1) * 128)
            hi, lo = split(ci * cb - si * sb)
            thi[0:NF, cols] = hi
            tlo[0:NF, cols] = lo
            hi, lo = split(-(si * cb + ci * sb))
            thi[NF : 2 * NF, cols] = hi
            tlo[NF : 2 * NF, cols] = lo

    def remote(src, dst, send, recv, device):
        return pltpu.make_async_remote_copy(
            src_ref=src, dst_ref=dst, send_sem=send, recv_sem=recv, device_id=device, device_id_type=MESH
        )

    opp, nxt, prv = (y + 2) % 4, (y + 1) % 4, (y + 3) % 4

    def copy(name, i):
        r = pl.ds(i * CH, CH)
        table = {
            "a1": (part.at[opp, 0, :, r], y1a.at[:, r], y1s.at[0, i], y1r.at[0, i], right),
            "b1": (part.at[opp, 1, :, r], y1b.at[:, r], y1s.at[1, i], y1r.at[1, i], left),
            "l1": (part.at[nxt, 1, :, r], y2l.at[1, :, r], y2s.at[0, i], y2rs.at[0, i], right),
            "r0": (part.at[prv, 0, :, r], y2r.at[0, :, r], y2s.at[1, i], y2rs.at[1, i], left),
            "l0": (part.at[nxt, 0, :, r], y2l.at[0, :, r], y2s.at[2, i], y2rs.at[2, i], right),
            "r1": (part.at[prv, 1, :, r], y2r.at[1, :, r], y2s.at[3, i], y2rs.at[3, i], left),
            "z": (part.at[y, 1 - zl, :, r], zrv.at[:, r], zs.at[i], zr.at[i], pair),
            "g": (part.at[y, 1 - zl, :, r], zgrv.at[:, r], zgs.at[i], zgr.at[i], cross),
            "h": (res.at[:, r], zhrv.at[:, r], zhs.at[i], zhr.at[i], far),
        }
        return remote(*table[name])

    def zcopy(name, i):
        r = pl.ds(i * CH, CH)
        rz = pl.ds((i - LAST * PG) * CH, CH)
        table = {
            "zz": (part.at[:, 1 - zl, :, r], zzrv.at[:, :, rz], zs.at[i], zr.at[i], pair),
            "a1": (part.at[opp, zl, 0, r], y1a.at[0, r], y1s.at[0, i], y1r.at[0, i], right),
            "b1": (part.at[opp, zl, 1, r], y1b.at[0, r], y1s.at[1, i], y1r.at[1, i], left),
            "l1": (part.at[nxt, zl, 1, r], y2l.at[0, 1, r], y2s.at[0, i], y2rs.at[0, i], right),
            "r0": (part.at[prv, zl, 0, r], y2r.at[0, 0, r], y2s.at[1, i], y2rs.at[1, i], left),
            "l0": (part.at[nxt, zl, 0, r], y2l.at[0, 0, r], y2s.at[2, i], y2rs.at[2, i], right),
            "r1": (part.at[prv, zl, 1, r], y2r.at[0, 1, r], y2s.at[3, i], y2rs.at[3, i], left),
        }
        return remote(*table[name])

    def forward_half(h):
        def tile(m, _):
            xs_ = tr[0, pl.ds(m * 32, 32), 8 * h : 8 * h + 8].reshape(32 * 8, NT)
            v = jnp.dot(xs_, ft[...], preferred_element_type=F32)
            for q in range(4):
                for n in range(32):
                    at = pl.ds(pl.multiple_of((m * 32 + n) * G + 8 * h, 8), 8)
                    spec[q, at, :] = v[n * 8 : n * 8 + 8, q * 128 : (q + 1) * 128]
            return 0

        lax.fori_loop(0, SL // 32, tile, 0)

    def forward(g):
        load(g).wait()

        def tile(m, _):
            xs_ = tr[g, pl.ds(m * 16, 16)].reshape(16 * G, NT)
            v = jnp.dot(xs_, ft[...], preferred_element_type=F32)
            for q in range(4):
                spec[q, pl.ds(pl.multiple_of(m * 16 * G, 16 * G), 16 * G), :] = v[
                    :, q * 128 : (q + 1) * 128
                ]
            return 0

        lax.fori_loop(0, SL // 16, tile, 0)

    def encode(i):
        for j in range(CH):
            at = pl.ds((i % PG) * CH + j, SL, stride=G)
            re = jnp.concatenate([spec[0, at, :], spec[1, at, :]], axis=1)
            im = jnp.concatenate([spec[2, at, :], spec[3, at, :]], axis=1)
            hi, lo = split(jnp.concatenate([re, im], axis=0))
            both = jnp.dot(
                code[...], jnp.concatenate([hi, lo], axis=0), preferred_element_type=F32
            )
            part[:, :, :, i * CH + j] = (both[0:128] + both[128:256]).reshape(NY, 2, 2, ET, NF)

    def inverse(one, two, i, which):
        r = pl.ds(i * CH, CH)
        v = [(one[c, r] + two[c, r]).reshape(CH * ET, NF) for c in range(2)]
        v = jnp.concatenate(v, axis=1)
        hi, lo = split(v)
        hl = jnp.concatenate([hi, lo], axis=0)
        n = CH * ET
        for xx in range(NX):
            cols = slice(xx * 256, (xx + 1) * 256)
            both = jnp.dot(hl, thi[:, cols], preferred_element_type=F32)
            o = both[0:n] + both[n : 2 * n] + jnp.dot(hi, tlo[:, cols], preferred_element_type=F32)
            for c in range(2):
                obuf[xx, c, pl.ds(which * RL + i * CH, CH)] = o[:, c * 128 : (c + 1) * 128].reshape(
                    CH, ET, 128
                )
        from_rcv = x * 4 + core + 2 * (zh if which == 0 else 1 - zh)
        dst = out.at[pl.ds(from_rcv * RL + i * CH, CH)]
        rows_ = pl.ds(which * RL + i * CH, CH)
        for dx, dc in others:
            xx, c, device = owner(dx, dc)
            remote(
                obuf.at[xx, c, rows_], dst, xs.at[xx * 2 + c], xr.at[x * 2 + core], device
            ).start()
        pltpu.make_async_copy(obuf.at[x, core, rows_], dst, own_sem).start()

    def less_observed(k):
        for p in range(2):
            for j in range(CH):
                at = k * CH + j
                rows = pl.ds(p * RL + at, ET, stride=2 * RL)
                seen = jnp.concatenate([obs[0, rows, :], obs[1, rows, :]], axis=1)
                res[p, at] = res[p, at] - seen

    def done(i, steps):
        n = 0
        for at in sorted(set(steps)):
            n = n + jnp.where(i >= at, steps.count(at), 0)
        return n

    def chunk(p):
        c = p
        for at in range(1, NCH):
            jump = SEQ[at] - SEQ[at - 1] - 1
            if jump:
                c = c + jnp.where(p >= at, jump, 0)
        return c

    def early(c):
        hit = c == ZS[0]
        for other in ZS[1:]:
            hit = hit | (c == other)
        return hit

    def stage0(p):
        c = chunk(p)
        z = early(c)

        @pl.when(c < LAST * PG)
        def _():
            @pl.when(c == 0)
            def _():
                forward_half(0)

            @pl.when((c > 0) & (c % PG == 0))
            def _():
                forward(c // PG)

            @pl.when((c % PG == 0) | (c == 1))
            def _():
                encode(c)

            @pl.when((c > 1) & (c % PG == 1))
            def _():
                lax.fori_loop(c, c + PG - 1, lambda k, _: (encode(k), 0)[1], 0)

        @pl.when(p == 0)
        def _():
            pl.semaphore_wait(barrier, len(partners))

        @pl.when(jnp.logical_not(z))
        def _():
            for name in ("a1", "b1", "l1", "r0"):
                copy(name, c).start()

        @pl.when(z)
        def _():
            zcopy("zz", c).wait_recv()
            r = pl.ds(c * CH, CH)
            part[:, zl, :, r] = part[:, zl, :, r] + zzrv[:, :, pl.ds((c - LAST * PG) * CH, CH)]
            for name in ("a1", "b1", "l1", "r0"):
                zcopy(name, c).start()

    def stage1(p, _):
        c = chunk(p)
        z = early(c)
        r = pl.ds(c * CH, CH)

        @pl.when(jnp.logical_not(z))
        def _():
            copy("a1", c).wait_recv()
            part[nxt, 0, :, r] = part[nxt, 0, :, r] + y1a[:, r]
            copy("l0", c).start()
            copy("b1", c).wait_recv()
            part[prv, 1, :, r] = part[prv, 1, :, r] + y1b[:, r]
            copy("r1", c).start()

        @pl.when(z)
        def _():
            zcopy("a1", c).wait_recv()
            part[nxt, zl, 0, r] = part[nxt, zl, 0, r] + y1a[0, r]
            zcopy("l0", c).start()
            zcopy("b1", c).wait_recv()
            part[prv, zl, 1, r] = part[prv, zl, 1, r] + y1b[0, r]
            zcopy("r1", c).start()

        return 0

    def stage2(p, _):
        c = chunk(p)
        z = early(c)
        r = pl.ds(c * CH, CH)

        @pl.when(jnp.logical_not(z))
        def _():
            for name in ("l1", "r0", "l0", "r1"):
                copy(name, c).wait_recv()
            part[y, 1 - zl, :, r] = part[y, 1 - zl, :, r] + y2l[1 - zl, :, r] + y2r[1 - zl, :, r]
            copy("z", c).start()
            copy("g", c).start()
            res[:, r] = part[y, zl, :, r] + y2l[zl, :, r] + y2r[zl, :, r]

        @pl.when(z)
        def _():
            for name in ("l1", "r0", "l0", "r1"):
                zcopy(name, c).wait_recv()
            res[:, r] = part[y, zl, :, r] + y2l[0, :, r] + y2r[0, :, r]
            zrv[:, r] = jnp.zeros((2, CH, ET, NF), F32)
            zgrv[:, r] = jnp.zeros((2, CH, ET, NF), F32)

        less_observed(c)
        copy("h", c).start()
        return 0

    def stage3(p, _):
        c = chunk(p)

        @pl.when(jnp.logical_not(early(c)))
        def _():
            copy("z", c).wait_recv()

        inverse(res, zrv, c, 0)
        return 0

    def stage4(p, _):
        c = chunk(p)

        @pl.when(jnp.logical_not(early(c)))
        def _():
            copy("g", c).wait_recv()

        copy("h", c).wait_recv()
        inverse(zhrv, zgrv, c, 1)
        return 0

    def step(i, _):
        @pl.when(i < NCH)
        def _():
            stage0(i)

        @pl.when(i == 2)
        def _():
            inverse_table()
            for h in range(2):
                load_observed(h).wait()

        @pl.when(i == ZG)
        def _():
            forward_half(1)
            lax.fori_loop(2, PG, lambda k, _: (encode(k), 0)[1], 0)
            forward(LAST)
            lax.fori_loop(LAST * PG, NCH, lambda k, _: (encode(k), 0)[1], 0)

        for at, c in zip(ZAT, ZS):
            @pl.when(i == at)
            def _(c=c):
                zcopy("zz", c).start()

        for stage, steps in zip((stage1, stage2, stage3, stage4), STEPS):
            lax.fori_loop(done(i - 1, steps), done(i, steps), stage, 0)
        return 0

    lax.fori_loop(0, STEPS[3][-1] + 1, step, 0)

    def drain(c, _):
        z = early(c)

        @pl.when(jnp.logical_not(z))
        def _():
            for name in ("a1", "b1", "l1", "r0", "l0", "r1", "z", "g"):
                copy(name, c).wait_send()

        @pl.when(z)
        def _():
            for name in ("a1", "b1", "l1", "r0", "l0", "r1", "zz"):
                zcopy(name, c).wait_send()

        copy("h", c).wait_send()
        return 0

    lax.fori_loop(0, NCH, drain, 0)
    whole = out.at[pl.ds(0, 2 * RL)]
    pltpu.make_async_copy(obuf.at[x, core], whole, own_sem).wait()
    for dx, dc in others:
        xx, c, device = owner(dx, dc)
        both = remote(obuf.at[xx, c], whole, xs.at[xx * 2 + c], xr.at[xx * 2 + c], device)
        both.wait_send()
        both.wait_recv()


def turn(rows, out, held, sem):
    def put(e):
        return pltpu.make_async_copy(held.at[e], out.at[e], sem.at[e])

    for e in range(ET):
        def some(m, _):
            at = pl.multiple_of(m * 128, 128)
            held[e, pl.ds(at, 128), :] = rows[pl.ds(at * ET + e, 128, stride=ET), :]
            return 0

        lax.fori_loop(0, 16 * RL // 128, some, 0)
        put(e).start()
    for e in range(ET):
        put(e).wait()


def body(traces, phases, bins, observed):
    dma = pltpu.SemaphoreType.DMA
    vmem = lambda *s: pltpu.VMEM(s, F32)
    hbm = pl.BlockSpec(memory_space=pltpu.HBM)
    flops = 2 * (SL * RL * NT * 2 * NF + 4 * 128 * 128 * RL * NF + 3 * 1024 * 512 * 1024)
    arrays = (traces, phases, bins.reshape(1, NF), observed.reshape(ET * 2 * RL, NF))
    rows = pl.pallas_call(
        kernel,
        out_shape=pltpu.VMEM((16 * RL, ET, 128), F32),
        in_specs=[hbm, hbm, hbm, hbm],
        out_specs=pl.BlockSpec(memory_space=pl.ANY),
        scratch_shapes=[
            pltpu.VMEM((RL // G, SL, G, NT), BF16),
            pltpu.VMEM((NT, 2 * NF), BF16),
            pltpu.VMEM((256, 256), BF16),
            vmem(4, SL * G, 128),
            vmem(NY, 2, 2, RL, ET, NF),
            vmem(2, RL, ET, NF),
            vmem(2, RL, ET, NF),
            vmem(2, 2, RL, ET, NF),
            vmem(2, 2, RL, ET, NF),
            vmem(2, RL, ET, NF),
            vmem(NY, 2, G, ET, NF),
            vmem(2, RL, ET, NF),
            vmem(2, RL, ET, NF),
            vmem(2, RL, ET, NF),
            pltpu.VMEM((2 * NF, 1024), BF16),
            pltpu.VMEM((2 * NF, 1024), BF16),
            vmem(NX, 2, 2 * RL, ET, 128),
            vmem(4, 128, NF),
            vmem(2, ET * 2 * RL, 128),
            pltpu.VMEM((SL, NE), jnp.int32),
            pltpu.VMEM((1, NF), jnp.int32),
            dma((RL // G,)),
            dma((2,)),
            dma((2,)),
            dma,
            dma((2, NCH)),
            dma((2, NCH)),
            dma((4, NCH)),
            dma((4, NCH)),
            dma((NCH,)),
            dma((NCH,)),
            dma((NCH,)),
            dma((NCH,)),
            dma((NCH,)),
            dma((NCH,)),
            dma((8,)),
            dma((8,)),
        ],
        compiler_params=pltpu.CompilerParams(
            collective_id=0, has_side_effects=True, vmem_limit_bytes=51 * 2**20
        ),
        cost_estimate=pl.CostEstimate(flops=flops, bytes_accessed=22 * 2**20, transcendentals=0),
    )(*(pltpu.with_memory_space_constraint(a, pltpu.HBM) for a in arrays))
    return pl.pallas_call(
        turn,
        out_shape=jax.ShapeDtypeStruct((ET, 16 * RL, 128), F32),
        in_specs=[pl.BlockSpec(memory_space=pltpu.VMEM)],
        out_specs=pl.BlockSpec(memory_space=pl.ANY),
        scratch_shapes=[vmem(ET, 16 * RL, 128), dma((ET,))],
        compiler_params=pltpu.CompilerParams(vmem_limit_bytes=16 * 2**20),
        cost_estimate=pl.CostEstimate(flops=0, bytes_accessed=8 * 2**20, transcendentals=0),
    )(pltpu.with_memory_space_constraint(rows.reshape(16 * RL * ET, 128), pltpu.VMEM))


def solution(mesh):
    in_specs = (P("shot", "rcv", None), P("shot", None), P(), P("shot", None, "rcv", None))
    out_specs = P("shot", None, "rcv")
    return jax.shard_map(body, mesh=mesh, in_specs=in_specs, out_specs=out_specs, check_vma=False)
```

```python
import functools
import math

import jax
import jax.numpy as jnp
from jax import lax
from jax.experimental import pallas as pl
from jax.experimental.pallas import tpu as pltpu
from jax.sharding import PartitionSpec as P

MESH = pl.DeviceIdType.MESH
F32 = jnp.float32
BF16 = jnp.bfloat16

NT = 2048
NF = 256
SL = 64
RL = 64
NE = 64
G = 16
CH = 4
NCH = RL // CH
ZS = (12, 13, 14)
SEQ = (0, 1, 2, 3, 4, 5, 6, 12, 7, 8, 13, 9, 10, 14, 11, 15)
PG = G // CH
LAST = RL // G - 1
STEPS = (
    (1, 1, 4, 4, 4, 6, 7, 9, 10, 11, 11, 12, 13, 14, 19, 23),
    (2, 4, 5, 5, 6, 8, 9, 11, 12, 12, 13, 14, 17, 21, 24, 25),
    (4, 5, 7, 7, 10, 10, 11, 11, 12, 13, 13, 17, 21, 21, 25, 26),
    (4, 7, 7, 10, 10, 10, 11, 12, 15, 15, 18, 21, 24, 24, 25, 26),
)
ZG = (1, 3)
ZAT = (1, 3, 10)
ET = 8
NX = 4
NY = 4


def trig(k):
    q = lax.shift_right_logical(k + 256, 9)
    x = (k - q * 512).astype(F32) * (2.0 * math.pi / NT)
    q = q & 3
    x2 = x * x
    s = x + x * x2 * (-1.0 / 6 + x2 * (1.0 / 120 + x2 * (-1.0 / 5040 + x2 * (1.0 / 362880))))
    c = 1.0 + x2 * (-0.5 + x2 * (1.0 / 24 + x2 * (-1.0 / 720 + x2 * (1.0 / 40320 - x2 * (1.0 / 3628800)))))
    odd = (q & 1) == 1
    cos = jnp.where(odd, s, c)
    sin = jnp.where(odd, c, s)
    cos = jnp.where((q == 1) | (q == 2), -cos, cos)
    sin = jnp.where(q >= 2, -sin, sin)
    return cos, sin


def split(v):
    hi = v.astype(BF16)
    lo = (v - hi.astype(F32)).astype(BF16)
    return hi, lo


def kernel(
    traces, phases, bins, observed, out,
    tr, ft, code, spec, part, y1a, y1b, y2l, y2r, zrv, zzrv, res, zhrv, zgrv, thi, tlo, obuf, base, obs,
    ph, bn, tr_sem, obs_sem, in_sem, own_sem, y1s, y1r, y2s, y2rs, zs, zr, zhs, zhr, zgs, zgr, xs, xr,
):
    shot = lax.axis_index("shot")
    rcv = lax.axis_index("rcv")
    y = shot % 4
    zl = shot // 4
    x = rcv // 4
    zh = (rcv // 2) % 2
    core = rcv % 2

    def at_y(d):
        return {"shot": zl * 4 + (y + d + 4) % 4, "rcv": rcv}

    left, right = at_y(-1), at_y(1)
    pair = {"shot": (1 - zl) * 4 + y, "rcv": rcv}
    far = {"shot": shot, "rcv": x * 4 + (1 - zh) * 2 + core}
    cross = {"shot": (1 - zl) * 4 + y, "rcv": x * 4 + (1 - zh) * 2 + core}

    def owner(dx, dc):
        xx, cc = (x + dx) % 4, (core + dc) % 2
        return xx, cc, {"shot": shot, "rcv": xx * 4 + zh * 2 + cc}

    others = [(dx, dc) for dx in (2, 1, 3, 0) for dc in (0, 1) if (dx, dc) != (0, 0)]

    def load(g):
        return pltpu.make_async_copy(traces.at[:, pl.ds(g * G, G), :], tr.at[g], tr_sem.at[g])

    def load_observed(h):
        return pltpu.make_async_copy(
            observed.at[:, pl.ds(h * 128, 128)], obs.at[h], obs_sem.at[h]
        )

    load_phases = pltpu.make_async_copy(phases, ph, in_sem.at[0])
    load_bins = pltpu.make_async_copy(bins, bn, in_sem.at[1])
    load_bins.start()
    load_phases.start()
    load(0).start()

    barrier = pltpu.get_barrier_semaphore()
    partners = [left, right, pair, far, cross] + [owner(dx, dc)[2] for dx, dc in others]
    for d in partners:
        pl.semaphore_signal(barrier, inc=1, device_id=d, device_id_type=MESH)

    load_phases.wait()
    cc, cs = trig(ph[...] * 32)
    cc, cs = cc * (1.0 / 1024), cs * (1.0 / 1024)
    mat = jnp.concatenate(
        [jnp.concatenate([cc, cs], axis=1), jnp.concatenate([-cs, cc], axis=1)], axis=0
    ).T
    rows = []
    for yy in range(NY):
        for zz in range(2):
            for c in range(2):
                at = c * NE + zz * 32 + yy * 8
                rows.append(mat[at : at + 8, :])
    mat = jnp.concatenate(rows, axis=0)
    chi, clo = split(mat)
    code[...] = jnp.concatenate(
        [jnp.concatenate([chi, chi], axis=1), jnp.concatenate([clo, clo], axis=1)], axis=0
    )

    row = lax.broadcasted_iota(jnp.int32, (128, NF), 0)
    load_bins.wait()
    b = jnp.broadcast_to(bn[...], (128, NF))
    cosb, sinb = trig((row * b) & (NT - 1))
    base[0] = cosb
    base[1] = sinb
    row8 = lax.broadcasted_iota(jnp.int32, (8, NF), 0)
    cosa, sina = trig((row8 * 128 * b[:8]) & (NT - 1))
    base[2, 0:8] = cosa
    base[3, 0:8] = sina

    def forward_rows(a, _):
        ca, sa = base[2, pl.ds(a, 1), :], -base[3, pl.ds(a, 1), :]
        cb, sb = base[0], base[1]
        at = pl.ds(pl.multiple_of(a * 128, 128), 128)
        half = pl.ds(pl.multiple_of(a * 128 + NT // 2, 128), 128)
        cos = ca * cb + sa * sb
        sin = sa * cb - ca * sb
        ft[at, 0:NF] = cos.astype(BF16)
        ft[half, 0:NF] = (cos * flip).astype(BF16)
        ft[at, NF : 2 * NF] = sin.astype(BF16)
        ft[half, NF : 2 * NF] = (sin * flip).astype(BF16)
        return 0

    flip = (1 - 2 * (b[0:1] & 1)).astype(F32)
    lax.fori_loop(0, 8, forward_rows, 0)
    load(0).wait()
    for g in (LAST, *range(1, LAST)):
        load(g).start()
    for h in range(2):
        load_observed(h).start()

    def inverse_table():
        scale = 1.0 / math.sqrt(2 * NF)
        blk = lax.broadcasted_iota(jnp.int32, (128, NF), 0)
        blk = ((blk // 2) * 4 + zh * 2 + blk % 2) & 15
        ca, sa = trig((blk * 128 * b) & (NT - 1))
        ca, sa = (ca * scale).T, (sa * scale).T
        cb, sb = base[0].T, base[1].T
        for i in range(2 * NX):
            ci, si = ca[:, i : i + 1], sa[:, i : i + 1]
            cols = slice(i * 128, (i + 1) * 128)
            hi, lo = split(ci * cb - si * sb)
            thi[0:NF, cols] = hi
            tlo[0:NF, cols] = lo
            hi, lo = split(-(si * cb + ci * sb))
            thi[NF : 2 * NF, cols] = hi
            tlo[NF : 2 * NF, cols] = lo

    def remote(src, dst, send, recv, device):
        return pltpu.make_async_remote_copy(
            src_ref=src, dst_ref=dst, send_sem=send, recv_sem=recv, device_id=device, device_id_type=MESH
        )

    opp, nxt, prv = (y + 2) % 4, (y + 1) % 4, (y + 3) % 4

    def copy(name, i):
        r = pl.ds(i * CH, CH)
        table = {
            "a1": (part.at[opp, 0, :, r], y1a.at[:, r], y1s.at[0, i], y1r.at[0, i], right),
            "b1": (part.at[opp, 1, :, r], y1b.at[:, r], y1s.at[1, i], y1r.at[1, i], left),
            "l1": (part.at[nxt, 1, :, r], y2l.at[1, :, r], y2s.at[0, i], y2rs.at[0, i], right),
            "r0": (part.at[prv, 0, :, r], y2r.at[0, :, r], y2s.at[1, i], y2rs.at[1, i], left),
            "l0": (part.at[nxt, 0, :, r], y2l.at[0, :, r], y2s.at[2, i], y2rs.at[2, i], right),
            "r1": (part.at[prv, 1, :, r], y2r.at[1, :, r], y2s.at[3, i], y2rs.at[3, i], left),
            "z": (part.at[y, 1 - zl, :, r], zrv.at[:, r], zs.at[i], zr.at[i], pair),
            "g": (part.at[y, 1 - zl, :, r], zgrv.at[:, r], zgs.at[i], zgr.at[i], cross),
            "h": (res.at[:, r], zhrv.at[:, r], zhs.at[i], zhr.at[i], far),
        }
        return remote(*table[name])

    def zcopy(name, i):
        r = pl.ds(i * CH, CH)
        rz = pl.ds((i - LAST * PG) * CH, CH)
        table = {
            "zz": (part.at[:, 1 - zl, :, r], zzrv.at[:, :, rz], zs.at[i], zr.at[i], pair),
            "a1": (part.at[opp, zl, 0, r], y1a.at[0, r], y1s.at[0, i], y1r.at[0, i], right),
            "b1": (part.at[opp, zl, 1, r], y1b.at[0, r], y1s.at[1, i], y1r.at[1, i], left),
            "l1": (part.at[nxt, zl, 1, r], y2l.at[0, 1, r], y2s.at[0, i], y2rs.at[0, i], right),
            "r0": (part.at[prv, zl, 0, r], y2r.at[0, 0, r], y2s.at[1, i], y2rs.at[1, i], left),
            "l0": (part.at[nxt, zl, 0, r], y2l.at[0, 0, r], y2s.at[2, i], y2rs.at[2, i], right),
            "r1": (part.at[prv, zl, 1, r], y2r.at[0, 1, r], y2s.at[3, i], y2rs.at[3, i], left),
        }
        return remote(*table[name])

    def forward(g, h):
        def tile(m, _):
            xs_ = tr[g, pl.ds(m * 32, 32), 8 * h : 8 * h + 8].reshape(32 * 8, NT)
            v = jnp.dot(xs_, ft[...], preferred_element_type=F32)
            for q in range(4):
                for n in range(32):
                    at = pl.ds(pl.multiple_of((m * 32 + n) * G + 8 * h, 8), 8)
                    spec[q, at, :] = v[n * 8 : n * 8 + 8, q * 128 : (q + 1) * 128]
            return 0

        lax.fori_loop(0, SL // 32, tile, 0)

    def encode_two(k):
        lax.fori_loop(k, k + 2, lambda n, _: (encode(n), 0)[1], 0)

    def encode(i):
        for j in range(CH):
            at = pl.ds((i % PG) * CH + j, SL, stride=G)
            re = jnp.concatenate([spec[0, at, :], spec[1, at, :]], axis=1)
            im = jnp.concatenate([spec[2, at, :], spec[3, at, :]], axis=1)
            hi, lo = split(jnp.concatenate([re, im], axis=0))
            both = jnp.dot(
                code[...], jnp.concatenate([hi, lo], axis=0), preferred_element_type=F32
            )
            part[:, :, :, i * CH + j] = (both[0:128] + both[128:256]).reshape(NY, 2, 2, ET, NF)

    def inverse(one, two, i, which):
        r = pl.ds(i * CH, CH)
        v = [(one[c, r] + two[c, r]).reshape(CH * ET, NF) for c in range(2)]
        v = jnp.concatenate(v, axis=1)
        hi, lo = split(v)
        hl = jnp.concatenate([hi, lo], axis=0)
        n = CH * ET
        for xx in range(NX):
            cols = slice(xx * 256, (xx + 1) * 256)
            both = jnp.dot(hl, thi[:, cols], preferred_element_type=F32)
            o = both[0:n] + both[n : 2 * n] + jnp.dot(hi, tlo[:, cols], preferred_element_type=F32)
            for c in range(2):
                obuf[xx, c, pl.ds(which * RL + i * CH, CH)] = o[:, c * 128 : (c + 1) * 128].reshape(
                    CH, ET, 128
                )
        from_rcv = x * 4 + core + 2 * (zh if which == 0 else 1 - zh)
        dst = out.at[pl.ds(from_rcv * RL + i * CH, CH)]
        rows_ = pl.ds(which * RL + i * CH, CH)
        for dx, dc in others:
            xx, c, device = owner(dx, dc)
            remote(
                obuf.at[xx, c, rows_], dst, xs.at[xx * 2 + c], xr.at[x * 2 + core], device
            ).start()
        pltpu.make_async_copy(obuf.at[x, core, rows_], dst, own_sem).start()

    def less_observed(k):
        for p in range(2):
            for j in range(CH):
                at = k * CH + j
                rows = pl.ds(p * RL + at, ET, stride=2 * RL)
                seen = jnp.concatenate([obs[0, rows, :], obs[1, rows, :]], axis=1)
                res[p, at] = res[p, at] - seen

    def done(i, steps):
        n = 0
        for at in sorted(set(steps)):
            n = n + jnp.where(i >= at, steps.count(at), 0)
        return n

    def chunk(p):
        c = p
        for at in range(1, NCH):
            jump = SEQ[at] - SEQ[at - 1] - 1
            if jump:
                c = c + jnp.where(p >= at, jump, 0)
        return c

    def early(c):
        hit = c == ZS[0]
        for other in ZS[1:]:
            hit = hit | (c == other)
        return hit

    def stage0(p):
        c = chunk(p)
        z = early(c)

        @pl.when(c < LAST * PG)
        def _():
            @pl.when((c > 0) & (c % PG == 0))
            def _():
                load(c // PG).wait()

            @pl.when(c % PG == 0)
            def _():
                forward(c // PG, 0)

            @pl.when(c % PG < 2)
            def _():
                encode(c)

        @pl.when(p == 0)
        def _():
            pl.semaphore_wait(barrier, len(partners))

        @pl.when(jnp.logical_not(z))
        def _():
            for name in ("a1", "b1", "l1", "r0"):
                copy(name, c).start()

        @pl.when(z)
        def _():
            zcopy("zz", c).wait_recv()
            r = pl.ds(c * CH, CH)
            part[:, zl, :, r] = part[:, zl, :, r] + zzrv[:, :, pl.ds((c - LAST * PG) * CH, CH)]
            for name in ("a1", "b1", "l1", "r0"):
                zcopy(name, c).start()

        @pl.when((c < LAST * PG) & (c % PG == 1))
        def _():
            forward(c // PG, 1)
            encode_two(c + 1)

    def stage1(p, _):
        c = chunk(p)
        z = early(c)
        r = pl.ds(c * CH, CH)

        @pl.when(jnp.logical_not(z))
        def _():
            copy("a1", c).wait_recv()
            part[nxt, 0, :, r] = part[nxt, 0, :, r] + y1a[:, r]
            copy("l0", c).start()
            copy("b1", c).wait_recv()
            part[prv, 1, :, r] = part[prv, 1, :, r] + y1b[:, r]
            copy("r1", c).start()

        @pl.when(z)
        def _():
            zcopy("a1", c).wait_recv()
            part[nxt, zl, 0, r] = part[nxt, zl, 0, r] + y1a[0, r]
            zcopy("l0", c).start()
            zcopy("b1", c).wait_recv()
            part[prv, zl, 1, r] = part[prv, zl, 1, r] + y1b[0, r]
            zcopy("r1", c).start()

        return 0

    def stage2(p, _):
        c = chunk(p)
        z = early(c)
        r = pl.ds(c * CH, CH)

        @pl.when(jnp.logical_not(z))
        def _():
            for name in ("l1", "r0", "l0", "r1"):
                copy(name, c).wait_recv()
            part[y, 1 - zl, :, r] = part[y, 1 - zl, :, r] + y2l[1 - zl, :, r] + y2r[1 - zl, :, r]
            copy("z", c).start()
            copy("g", c).start()
            res[:, r] = part[y, zl, :, r] + y2l[zl, :, r] + y2r[zl, :, r]

        @pl.when(z)
        def _():
            for name in ("l1", "r0", "l0", "r1"):
                zcopy(name, c).wait_recv()
            res[:, r] = part[y, zl, :, r] + y2l[0, :, r] + y2r[0, :, r]
            zrv[:, r] = jnp.zeros((2, CH, ET, NF), F32)
            zgrv[:, r] = jnp.zeros((2, CH, ET, NF), F32)

        less_observed(c)
        copy("h", c).start()
        return 0

    def stage3(p, _):
        c = chunk(p)

        @pl.when(jnp.logical_not(early(c)))
        def _():
            copy("z", c).wait_recv()

        inverse(res, zrv, c, 0)
        return 0

    def stage4(p, _):
        c = chunk(p)

        @pl.when(jnp.logical_not(early(c)))
        def _():
            copy("g", c).wait_recv()

        copy("h", c).wait_recv()
        inverse(zhrv, zgrv, c, 1)
        return 0

    def step(i, _):
        @pl.when(i < NCH)
        def _():
            stage0(i)

        @pl.when(i == 2)
        def _():
            inverse_table()
            for h in range(2):
                load_observed(h).wait()

        @pl.when(i == ZG[0])
        def _():
            load(LAST).wait()
            forward(LAST, 0)
            encode_two(LAST * PG)

        @pl.when(i == ZG[1])
        def _():
            forward(LAST, 1)
            encode_two(LAST * PG + 2)

        for at, c in zip(ZAT, ZS):
            @pl.when(i == at)
            def _(c=c):
                zcopy("zz", c).start()

        for stage, steps in zip((stage1, stage2, stage3, stage4), STEPS):
            lax.fori_loop(done(i - 1, steps), done(i, steps), stage, 0)
        return 0

    lax.fori_loop(0, STEPS[3][-1] + 1, step, 0)

    def drain(c, _):
        z = early(c)

        @pl.when(jnp.logical_not(z))
        def _():
            for name in ("a1", "b1", "l1", "r0", "l0", "r1", "z", "g"):
                copy(name, c).wait_send()

        @pl.when(z)
        def _():
            for name in ("a1", "b1", "l1", "r0", "l0", "r1", "zz"):
                zcopy(name, c).wait_send()

        copy("h", c).wait_send()
        return 0

    lax.fori_loop(0, NCH, drain, 0)
    whole = out.at[pl.ds(0, 2 * RL)]
    pltpu.make_async_copy(obuf.at[x, core], whole, own_sem).wait()
    for dx, dc in others:
        xx, c, device = owner(dx, dc)
        both = remote(obuf.at[xx, c], whole, xs.at[xx * 2 + c], xr.at[xx * 2 + c], device)
        both.wait_send()
        both.wait_recv()


def turn(rows, out, held, sem):
    def put(e):
        return pltpu.make_async_copy(held.at[e], out.at[e], sem.at[e])

    for e in range(ET):
        def some(m, _):
            at = pl.multiple_of(m * 128, 128)
            held[e, pl.ds(at, 128), :] = rows[pl.ds(at * ET + e, 128, stride=ET), :]
            return 0

        lax.fori_loop(0, 16 * RL // 128, some, 0)
        put(e).start()
    for e in range(ET):
        put(e).wait()


def body(traces, phases, bins, observed):
    dma = pltpu.SemaphoreType.DMA
    vmem = lambda *s: pltpu.VMEM(s, F32)
    hbm = pl.BlockSpec(memory_space=pltpu.HBM)
    flops = 2 * (SL * RL * NT * 2 * NF + 4 * 128 * 128 * RL * NF + 3 * 1024 * 512 * 1024)
    arrays = (traces, phases, bins.reshape(1, NF), observed.reshape(ET * 2 * RL, NF))
    rows = pl.pallas_call(
        kernel,
        out_shape=pltpu.VMEM((16 * RL, ET, 128), F32),
        in_specs=[hbm, hbm, hbm, hbm],
        out_specs=pl.BlockSpec(memory_space=pl.ANY),
        scratch_shapes=[
            pltpu.VMEM((RL // G, SL, G, NT), BF16),
            pltpu.VMEM((NT, 2 * NF), BF16),
            pltpu.VMEM((256, 256), BF16),
            vmem(4, SL * G, 128),
            vmem(NY, 2, 2, RL, ET, NF),
            vmem(2, RL, ET, NF),
            vmem(2, RL, ET, NF),
            vmem(2, 2, RL, ET, NF),
            vmem(2, 2, RL, ET, NF),
            vmem(2, RL, ET, NF),
            vmem(NY, 2, G, ET, NF),
            vmem(2, RL, ET, NF),
            vmem(2, RL, ET, NF),
            vmem(2, RL, ET, NF),
            pltpu.VMEM((2 * NF, 1024), BF16),
            pltpu.VMEM((2 * NF, 1024), BF16),
            vmem(NX, 2, 2 * RL, ET, 128),
            vmem(4, 128, NF),
            vmem(2, ET * 2 * RL, 128),
            pltpu.VMEM((SL, NE), jnp.int32),
            pltpu.VMEM((1, NF), jnp.int32),
            dma((RL // G,)),
            dma((2,)),
            dma((2,)),
            dma,
            dma((2, NCH)),
            dma((2, NCH)),
            dma((4, NCH)),
            dma((4, NCH)),
            dma((NCH,)),
            dma((NCH,)),
            dma((NCH,)),
            dma((NCH,)),
            dma((NCH,)),
            dma((NCH,)),
            dma((8,)),
            dma((8,)),
        ],
        compiler_params=pltpu.CompilerParams(
            collective_id=0, has_side_effects=True, vmem_limit_bytes=51 * 2**20
        ),
        cost_estimate=pl.CostEstimate(flops=flops, bytes_accessed=22 * 2**20, transcendentals=0),
    )(*(pltpu.with_memory_space_constraint(a, pltpu.HBM) for a in arrays))
    return pl.pallas_call(
        turn,
        out_shape=jax.ShapeDtypeStruct((ET, 16 * RL, 128), F32),
        in_specs=[pl.BlockSpec(memory_space=pltpu.VMEM)],
        out_specs=pl.BlockSpec(memory_space=pl.ANY),
        scratch_shapes=[vmem(ET, 16 * RL, 128), dma((ET,))],
        compiler_params=pltpu.CompilerParams(vmem_limit_bytes=16 * 2**20),
        cost_estimate=pl.CostEstimate(flops=0, bytes_accessed=8 * 2**20, transcendentals=0),
    )(pltpu.with_memory_space_constraint(rows.reshape(16 * RL * ET, 128), pltpu.VMEM))


def solution(mesh):
    in_specs = (P("shot", "rcv", None), P("shot", None), P(), P("shot", None, "rcv", None))
    out_specs = P("shot", None, "rcv")
    return jax.shard_map(body, mesh=mesh, in_specs=in_specs, out_specs=out_specs, check_vma=False)
```

```python
import functools
import math

import jax
import jax.numpy as jnp
from jax import lax
from jax.experimental import pallas as pl
from jax.experimental.pallas import tpu as pltpu
from jax.sharding import PartitionSpec as P

MESH = pl.DeviceIdType.MESH
F32 = jnp.float32
BF16 = jnp.bfloat16

NT = 2048
NF = 256
SL = 64
RL = 64
NE = 64
G = 16
CH = 4
NCH = RL // CH
ZS = (12, 13, 14)
SEQ = (0, 1, 2, 3, 4, 5, 6, 12, 7, 8, 13, 9, 10, 14, 11, 15)
PG = G // CH
LAST = RL // G - 1
STEPS = (
    (1, 1, 4, 4, 4, 6, 7, 9, 10, 11, 11, 12, 13, 14, 19, 23),
    (2, 4, 5, 5, 6, 8, 9, 11, 12, 12, 13, 14, 17, 21, 24, 25),
    (4, 5, 7, 7, 10, 10, 11, 11, 12, 13, 13, 17, 21, 21, 25, 26),
    (4, 7, 7, 10, 10, 10, 11, 12, 15, 15, 18, 21, 24, 24, 25, 26),
)
ZG = (1, 3)
ZAT = (1, 3, 10)
ET = 8
NX = 4
NY = 4


def trig(k):
    q = lax.shift_right_logical(k + 256, 9)
    x = (k - q * 512).astype(F32) * (2.0 * math.pi / NT)
    q = q & 3
    x2 = x * x
    s = x + x * x2 * (-1.0 / 6 + x2 * (1.0 / 120 + x2 * (-1.0 / 5040 + x2 * (1.0 / 362880))))
    c = 1.0 + x2 * (-0.5 + x2 * (1.0 / 24 + x2 * (-1.0 / 720 + x2 * (1.0 / 40320 - x2 * (1.0 / 3628800)))))
    odd = (q & 1) == 1
    cos = jnp.where(odd, s, c)
    sin = jnp.where(odd, c, s)
    cos = jnp.where((q == 1) | (q == 2), -cos, cos)
    sin = jnp.where(q >= 2, -sin, sin)
    return cos, sin


def split(v):
    hi = v.astype(BF16)
    lo = (v - hi.astype(F32)).astype(BF16)
    return hi, lo


def kernel(
    traces, phases, bins, observed, out,
    tr, ft, code, spec, part, y1a, y1b, y2l, y2r, zrv, zzrv, res, zhrv, zgrv, thi, tlo, obuf, base, obs,
    ph, bn, tr_sem, obs_sem, in_sem, own_sem, y1s, y1r, y2s, y2rs, zs, zr, zhs, zhr, zgs, zgr, xs, xr,
):
    shot = lax.axis_index("shot")
    rcv = lax.axis_index("rcv")
    y = shot % 4
    zl = shot // 4
    x = rcv // 4
    zh = (rcv // 2) % 2
    core = rcv % 2

    def at_y(d):
        return {"shot": zl * 4 + (y + d + 4) % 4, "rcv": rcv}

    left, right = at_y(-1), at_y(1)
    pair = {"shot": (1 - zl) * 4 + y, "rcv": rcv}
    far = {"shot": shot, "rcv": x * 4 + (1 - zh) * 2 + core}
    cross = {"shot": (1 - zl) * 4 + y, "rcv": x * 4 + (1 - zh) * 2 + core}

    def owner(dx, dc):
        xx, cc = (x + dx) % 4, (core + dc) % 2
        return xx, cc, {"shot": shot, "rcv": xx * 4 + zh * 2 + cc}

    others = [(dx, dc) for dx in (2, 1, 3, 0) for dc in (0, 1) if (dx, dc) != (0, 0)]

    def load(g):
        return pltpu.make_async_copy(traces.at[:, pl.ds(g * G, G), :], tr.at[g], tr_sem.at[g])

    def load_observed(h):
        return pltpu.make_async_copy(
            observed.at[:, pl.ds(h * 128, 128)], obs.at[h], obs_sem.at[h]
        )

    load_phases = pltpu.make_async_copy(phases, ph, in_sem.at[0])
    load_bins = pltpu.make_async_copy(bins, bn, in_sem.at[1])
    load_bins.start()
    load_phases.start()
    load(0).start()

    barrier = pltpu.get_barrier_semaphore()
    partners = [left, right, pair, far, cross] + [owner(dx, dc)[2] for dx, dc in others]
    for d in partners:
        pl.semaphore_signal(barrier, inc=1, device_id=d, device_id_type=MESH)

    load_phases.wait()
    cc, cs = trig(ph[...] * 32)
    cc, cs = cc * (1.0 / 1024), cs * (1.0 / 1024)
    mat = jnp.concatenate(
        [jnp.concatenate([cc, cs], axis=1), jnp.concatenate([-cs, cc], axis=1)], axis=0
    ).T
    rows = []
    for yy in range(NY):
        for zz in range(2):
            for c in range(2):
                at = c * NE + zz * 32 + yy * 8
                rows.append(mat[at : at + 8, :])
    mat = jnp.concatenate(rows, axis=0)
    chi, clo = split(mat)
    code[...] = jnp.concatenate(
        [jnp.concatenate([chi, chi], axis=1), jnp.concatenate([clo, clo], axis=1)], axis=0
    )

    row = lax.broadcasted_iota(jnp.int32, (128, NF), 0)
    load_bins.wait()
    b = jnp.broadcast_to(bn[...], (128, NF))
    cosb, sinb = trig((row * b) & (NT - 1))
    base[0] = cosb
    base[1] = sinb
    row8 = lax.broadcasted_iota(jnp.int32, (8, NF), 0)
    cosa, sina = trig((row8 * 128 * b[:8]) & (NT - 1))
    base[2, 0:8] = cosa
    base[3, 0:8] = sina

    def forward_rows(a, _):
        ca, sa = base[2, pl.ds(a, 1), :], -base[3, pl.ds(a, 1), :]
        cb, sb = base[0], base[1]
        at = pl.ds(pl.multiple_of(a * 128, 128), 128)
        half = pl.ds(pl.multiple_of(a * 128 + NT // 2, 128), 128)
        cos = ca * cb + sa * sb
        sin = sa * cb - ca * sb
        ft[at, 0:NF] = cos.astype(BF16)
        ft[half, 0:NF] = (cos * flip).astype(BF16)
        ft[at, NF : 2 * NF] = sin.astype(BF16)
        ft[half, NF : 2 * NF] = (sin * flip).astype(BF16)
        return 0

    flip = (1 - 2 * (b[0:1] & 1)).astype(F32)
    lax.fori_loop(0, 8, forward_rows, 0)
    load(0).wait()
    for g in (LAST, *range(1, LAST)):
        load(g).start()
    for h in range(2):
        load_observed(h).start()

    def inverse_table():
        scale = 1.0 / math.sqrt(2 * NF)
        blk = lax.broadcasted_iota(jnp.int32, (128, NF), 0)
        blk = ((blk // 2) * 4 + zh * 2 + blk % 2) & 15
        ca, sa = trig((blk * 128 * b) & (NT - 1))
        ca, sa = (ca * scale).T, (sa * scale).T
        cb, sb = base[0].T, base[1].T
        for i in range(2 * NX):
            ci, si = ca[:, i : i + 1], sa[:, i : i + 1]
            cols = slice(i * 128, (i + 1) * 128)
            hi, lo = split(ci * cb - si * sb)
            thi[0:NF, cols] = hi
            tlo[0:NF, cols] = lo
            hi, lo = split(-(si * cb + ci * sb))
            thi[NF : 2 * NF, cols] = hi
            tlo[NF : 2 * NF, cols] = lo

    def remote(src, dst, send, recv, device):
        return pltpu.make_async_remote_copy(
            src_ref=src, dst_ref=dst, send_sem=send, recv_sem=recv, device_id=device, device_id_type=MESH
        )

    opp, nxt, prv = (y + 2) % 4, (y + 1) % 4, (y + 3) % 4

    def copy(name, i):
        r = pl.ds(i * CH, CH)
        table = {
            "a1": (part.at[opp, 0, :, r], y1a.at[:, r], y1s.at[0, i], y1r.at[0, i], right),
            "b1": (part.at[opp, 1, :, r], y1b.at[:, r], y1s.at[1, i], y1r.at[1, i], left),
            "l1": (part.at[nxt, 1, :, r], y2l.at[1, :, r], y2s.at[0, i], y2rs.at[0, i], right),
            "r0": (part.at[prv, 0, :, r], y2r.at[0, :, r], y2s.at[1, i], y2rs.at[1, i], left),
            "l0": (part.at[nxt, 0, :, r], y2l.at[0, :, r], y2s.at[2, i], y2rs.at[2, i], right),
            "r1": (part.at[prv, 1, :, r], y2r.at[1, :, r], y2s.at[3, i], y2rs.at[3, i], left),
            "z": (part.at[y, 1 - zl, :, r], zrv.at[:, r], zs.at[i], zr.at[i], pair),
            "g": (part.at[y, 1 - zl, :, r], zgrv.at[:, r], zgs.at[i], zgr.at[i], cross),
            "h": (res.at[:, r], zhrv.at[:, r], zhs.at[i], zhr.at[i], far),
        }
        return remote(*table[name])

    def zcopy(name, i):
        r = pl.ds(i * CH, CH)
        rz = pl.ds((i - LAST * PG) * CH, CH)
        table = {
            "zz": (part.at[:, 1 - zl, :, r], zzrv.at[:, :, rz], zs.at[i], zr.at[i], pair),
            "a1": (part.at[opp, zl, 0, r], y1a.at[0, r], y1s.at[0, i], y1r.at[0, i], right),
            "b1": (part.at[opp, zl, 1, r], y1b.at[0, r], y1s.at[1, i], y1r.at[1, i], left),
            "l1": (part.at[nxt, zl, 1, r], y2l.at[0, 1, r], y2s.at[0, i], y2rs.at[0, i], right),
            "r0": (part.at[prv, zl, 0, r], y2r.at[0, 0, r], y2s.at[1, i], y2rs.at[1, i], left),
            "l0": (part.at[nxt, zl, 0, r], y2l.at[0, 0, r], y2s.at[2, i], y2rs.at[2, i], right),
            "r1": (part.at[prv, zl, 1, r], y2r.at[0, 1, r], y2s.at[3, i], y2rs.at[3, i], left),
        }
        return remote(*table[name])

    def forward(g, h):
        def tile(m, _):
            xs_ = tr[g, pl.ds(m * 32, 32), 8 * h : 8 * h + 8].reshape(32 * 8, NT)
            v = jnp.dot(xs_, ft[...], preferred_element_type=F32)
            for q in range(4):
                for n in range(32):
                    at = pl.ds(pl.multiple_of((m * 32 + n) * G + 8 * h, 8), 8)
                    spec[q, at, :] = v[n * 8 : n * 8 + 8, q * 128 : (q + 1) * 128]
            return 0

        lax.fori_loop(0, SL // 32, tile, 0)

    def encode_two(k):
        lax.fori_loop(k, k + 2, lambda n, _: (encode(n), 0)[1], 0)

    def encode(i):
        for j in range(CH):
            at = pl.ds((i % PG) * CH + j, SL, stride=G)
            re = jnp.concatenate([spec[0, at, :], spec[1, at, :]], axis=1)
            im = jnp.concatenate([spec[2, at, :], spec[3, at, :]], axis=1)
            hi, lo = split(jnp.concatenate([re, im], axis=0))
            both = jnp.dot(
                code[...], jnp.concatenate([hi, lo], axis=0), preferred_element_type=F32
            )
            part[:, :, :, i * CH + j] = (both[0:128] + both[128:256]).reshape(NY, 2, 2, ET, NF)

    def inverse(one, two, i, which):
        r = pl.ds(i * CH, CH)
        v = [(one[c, r] + two[c, r]).reshape(CH * ET, NF) for c in range(2)]
        v = jnp.concatenate(v, axis=1)
        hi, lo = split(v)
        hl = jnp.concatenate([hi, lo], axis=0)
        n = CH * ET
        for xx in range(NX):
            cols = slice(xx * 256, (xx + 1) * 256)
            both = jnp.dot(hl, thi[:, cols], preferred_element_type=F32)
            o = both[0:n] + both[n : 2 * n] + jnp.dot(hi, tlo[:, cols], preferred_element_type=F32)
            for c in range(2):
                obuf[xx, c, pl.ds(which * RL + i * CH, CH)] = o[:, c * 128 : (c + 1) * 128].reshape(
                    CH, ET, 128
                )
        from_rcv = x * 4 + core + 2 * (zh if which == 0 else 1 - zh)
        dst = out.at[pl.ds(from_rcv * RL + i * CH, CH)]
        rows_ = pl.ds(which * RL + i * CH, CH)
        for dx, dc in others:
            xx, c, device = owner(dx, dc)
            remote(
                obuf.at[xx, c, rows_], dst, xs.at[xx * 2 + c], xr.at[x * 2 + core], device
            ).start()
        pltpu.make_async_copy(obuf.at[x, core, rows_], dst, own_sem).start()

    def less_observed(k):
        for p in range(2):
            for j in range(CH):
                at = k * CH + j
                rows = pl.ds(p * RL + at, ET, stride=2 * RL)
                seen = jnp.concatenate([obs[0, rows, :], obs[1, rows, :]], axis=1)
                part[y, zl, p, at] = part[y, zl, p, at] - seen

    def done(i, steps):
        n = 0
        for at in sorted(set(steps)):
            n = n + jnp.where(i >= at, steps.count(at), 0)
        return n

    def chunk(p):
        c = p
        for at in range(1, NCH):
            jump = SEQ[at] - SEQ[at - 1] - 1
            if jump:
                c = c + jnp.where(p >= at, jump, 0)
        return c

    def early(c):
        hit = c == ZS[0]
        for other in ZS[1:]:
            hit = hit | (c == other)
        return hit

    def stage0(p):
        c = chunk(p)
        z = early(c)

        @pl.when(c < LAST * PG)
        def _():
            @pl.when((c > 0) & (c % PG == 0))
            def _():
                load(c // PG).wait()

            @pl.when(c % PG == 0)
            def _():
                forward(c // PG, 0)

            @pl.when(c % PG < 2)
            def _():
                encode(c)

        @pl.when(p == 0)
        def _():
            pl.semaphore_wait(barrier, len(partners))

        @pl.when(jnp.logical_not(z))
        def _():
            for name in ("a1", "b1", "l1", "r0"):
                copy(name, c).start()

        @pl.when(z)
        def _():
            zcopy("zz", c).wait_recv()
            r = pl.ds(c * CH, CH)
            part[:, zl, :, r] = part[:, zl, :, r] + zzrv[:, :, pl.ds((c - LAST * PG) * CH, CH)]
            for name in ("a1", "b1", "l1", "r0"):
                zcopy(name, c).start()

        @pl.when((c < LAST * PG) & (c % PG == 1))
        def _():
            forward(c // PG, 1)
            encode_two(c + 1)

    def stage1(p, _):
        c = chunk(p)
        z = early(c)
        less_observed(c)
        r = pl.ds(c * CH, CH)

        @pl.when(jnp.logical_not(z))
        def _():
            copy("a1", c).wait_recv()
            part[nxt, 0, :, r] = part[nxt, 0, :, r] + y1a[:, r]
            copy("l0", c).start()
            copy("b1", c).wait_recv()
            part[prv, 1, :, r] = part[prv, 1, :, r] + y1b[:, r]
            copy("r1", c).start()

        @pl.when(z)
        def _():
            zcopy("a1", c).wait_recv()
            part[nxt, zl, 0, r] = part[nxt, zl, 0, r] + y1a[0, r]
            zcopy("l0", c).start()
            zcopy("b1", c).wait_recv()
            part[prv, zl, 1, r] = part[prv, zl, 1, r] + y1b[0, r]
            zcopy("r1", c).start()

        return 0

    def stage2(p, _):
        c = chunk(p)
        z = early(c)
        r = pl.ds(c * CH, CH)

        @pl.when(jnp.logical_not(z))
        def _():
            for name in ("l1", "r0", "l0", "r1"):
                copy(name, c).wait_recv()
            part[y, 1 - zl, :, r] = part[y, 1 - zl, :, r] + y2l[1 - zl, :, r] + y2r[1 - zl, :, r]
            copy("z", c).start()
            copy("g", c).start()
            res[:, r] = part[y, zl, :, r] + y2l[zl, :, r] + y2r[zl, :, r]

        @pl.when(z)
        def _():
            for name in ("l1", "r0", "l0", "r1"):
                zcopy(name, c).wait_recv()
            res[:, r] = part[y, zl, :, r] + y2l[0, :, r] + y2r[0, :, r]
            zrv[:, r] = jnp.zeros((2, CH, ET, NF), F32)
            zgrv[:, r] = jnp.zeros((2, CH, ET, NF), F32)

        copy("h", c).start()
        return 0

    def stage3(p, _):
        c = chunk(p)

        @pl.when(jnp.logical_not(early(c)))
        def _():
            copy("z", c).wait_recv()

        inverse(res, zrv, c, 0)
        return 0

    def stage4(p, _):
        c = chunk(p)

        @pl.when(jnp.logical_not(early(c)))
        def _():
            copy("g", c).wait_recv()

        copy("h", c).wait_recv()
        inverse(zhrv, zgrv, c, 1)
        return 0

    def step(i, _):
        @pl.when(i < NCH)
        def _():
            stage0(i)

        @pl.when(i == 2)
        def _():
            inverse_table()

        @pl.when(i == ZG[0])
        def _():
            for h in range(2):
                load_observed(h).wait()
            load(LAST).wait()
            forward(LAST, 0)
            encode_two(LAST * PG)

        @pl.when(i == ZG[1])
        def _():
            forward(LAST, 1)
            encode_two(LAST * PG + 2)

        for at, c in zip(ZAT, ZS):
            @pl.when(i == at)
            def _(c=c):
                zcopy("zz", c).start()

        for stage, steps in zip((stage1, stage2, stage3, stage4), STEPS):
            lax.fori_loop(done(i - 1, steps), done(i, steps), stage, 0)
        return 0

    lax.fori_loop(0, STEPS[3][-1] + 1, step, 0)

    def drain(c, _):
        z = early(c)

        @pl.when(jnp.logical_not(z))
        def _():
            for name in ("a1", "b1", "l1", "r0", "l0", "r1", "z", "g"):
                copy(name, c).wait_send()

        @pl.when(z)
        def _():
            for name in ("a1", "b1", "l1", "r0", "l0", "r1", "zz"):
                zcopy(name, c).wait_send()

        copy("h", c).wait_send()
        return 0

    lax.fori_loop(0, NCH, drain, 0)
    whole = out.at[pl.ds(0, 2 * RL)]
    pltpu.make_async_copy(obuf.at[x, core], whole, own_sem).wait()
    for dx, dc in others:
        xx, c, device = owner(dx, dc)
        both = remote(obuf.at[xx, c], whole, xs.at[xx * 2 + c], xr.at[xx * 2 + c], device)
        both.wait_send()
        both.wait_recv()


def turn(rows, out, held, sem):
    def put(e):
        return pltpu.make_async_copy(held.at[e], out.at[e], sem.at[e])

    for e in range(ET):
        def some(m, _):
            at = pl.multiple_of(m * 128, 128)
            held[e, pl.ds(at, 128), :] = rows[pl.ds(at * ET + e, 128, stride=ET), :]
            return 0

        lax.fori_loop(0, 16 * RL // 128, some, 0)
        put(e).start()
    for e in range(ET):
        put(e).wait()


def body(traces, phases, bins, observed):
    dma = pltpu.SemaphoreType.DMA
    vmem = lambda *s: pltpu.VMEM(s, F32)
    hbm = pl.BlockSpec(memory_space=pltpu.HBM)
    flops = 2 * (SL * RL * NT * 2 * NF + 4 * 128 * 128 * RL * NF + 3 * 1024 * 512 * 1024)
    arrays = (traces, phases, bins.reshape(1, NF), observed.reshape(ET * 2 * RL, NF))
    rows = pl.pallas_call(
        kernel,
        out_shape=pltpu.VMEM((16 * RL, ET, 128), F32),
        in_specs=[hbm, hbm, hbm, hbm],
        out_specs=pl.BlockSpec(memory_space=pl.ANY),
        scratch_shapes=[
            pltpu.VMEM((RL // G, SL, G, NT), BF16),
            pltpu.VMEM((NT, 2 * NF), BF16),
            pltpu.VMEM((256, 256), BF16),
            vmem(4, SL * G, 128),
            vmem(NY, 2, 2, RL, ET, NF),
            vmem(2, RL, ET, NF),
            vmem(2, RL, ET, NF),
            vmem(2, 2, RL, ET, NF),
            vmem(2, 2, RL, ET, NF),
            vmem(2, RL, ET, NF),
            vmem(NY, 2, G, ET, NF),
            vmem(2, RL, ET, NF),
            vmem(2, RL, ET, NF),
            vmem(2, RL, ET, NF),
            pltpu.VMEM((2 * NF, 1024), BF16),
            pltpu.VMEM((2 * NF, 1024), BF16),
            vmem(NX, 2, 2 * RL, ET, 128),
            vmem(4, 128, NF),
            vmem(2, ET * 2 * RL, 128),
            pltpu.VMEM((SL, NE), jnp.int32),
            pltpu.VMEM((1, NF), jnp.int32),
            dma((RL // G,)),
            dma((2,)),
            dma((2,)),
            dma,
            dma((2, NCH)),
            dma((2, NCH)),
            dma((4, NCH)),
            dma((4, NCH)),
            dma((NCH,)),
            dma((NCH,)),
            dma((NCH,)),
            dma((NCH,)),
            dma((NCH,)),
            dma((NCH,)),
            dma((8,)),
            dma((8,)),
        ],
        compiler_params=pltpu.CompilerParams(
            collective_id=0, has_side_effects=True, vmem_limit_bytes=51 * 2**20
        ),
        cost_estimate=pl.CostEstimate(flops=flops, bytes_accessed=22 * 2**20, transcendentals=0),
    )(*(pltpu.with_memory_space_constraint(a, pltpu.HBM) for a in arrays))
    return pl.pallas_call(
        turn,
        out_shape=jax.ShapeDtypeStruct((ET, 16 * RL, 128), F32),
        in_specs=[pl.BlockSpec(memory_space=pltpu.VMEM)],
        out_specs=pl.BlockSpec(memory_space=pl.ANY),
        scratch_shapes=[vmem(ET, 16 * RL, 128), dma((ET,))],
        compiler_params=pltpu.CompilerParams(vmem_limit_bytes=16 * 2**20),
        cost_estimate=pl.CostEstimate(flops=0, bytes_accessed=8 * 2**20, transcendentals=0),
    )(pltpu.with_memory_space_constraint(rows.reshape(16 * RL * ET, 128), pltpu.VMEM))


def solution(mesh):
    in_specs = (P("shot", "rcv", None), P("shot", None), P(), P("shot", None, "rcv", None))
    out_specs = P("shot", None, "rcv")
    return jax.shard_map(body, mesh=mesh, in_specs=in_specs, out_specs=out_specs, check_vma=False)
```
